128 devices in a mesh: gx: 32 (over y, x, core), gy: 4 (over z).
Axes of the slice: x: 4, y: 4, z: 4, core: 2. Of those that a mesh axis runs over, the one named last changes fastest.
Arguments:
- hidden_in: bfloat16 [1024, 16384], P(('gx', 'gy')), may hold values from -6 to 6
- norm_gain: float32 [16384], replicated, may hold values from 0.1 to 1.9
- w_qkv: bfloat16 [16384, 18432], P('gy', 'gx'), may hold values from -0.046875 to 0.046875
- k_cache: bfloat16 [1024, 512, 1024], P(('gx', 'gy')), may hold values from -60 to 60
- v_cache: bfloat16 [1024, 512, 1024], P(('gx', 'gy')), may hold values from -6 to 6
- lengths: int32 [1024], P(('gx', 'gy')), may hold values from 1 to 512, as said below
- w_out: bfloat16 [16384, 16384], P('gy', 'gx'), may hold values from -0.375 to 0.375
Outputs:
- attn_out: bfloat16 [1024, 16384], P(('gx', 'gy'))
The draws below stay inside these ranges and needn't reach their ends.
Inputs may be any that keep to these rules, and one draw needn't show every extreme that they name: Row b attends to its first lengths[b] cached positions; some row has 512.
All inputs are finite; a program needn't handle non-finite values.
Results may differ from the reference program's by a relative error of at most 0.015.
The reference program's roundings to bfloat16 on the way count: a program that leaves them out, or rounds other values in their place, can miss the bound.
Values may be sent and summed in bfloat16 or wider, within the bound.
A program may use at most 128 MiB of HBM per device.

```python
import math
import jax
import jax.numpy as jnp
from jax import lax

D = 16384
HQ = 128
KVH = 8
HD = 128
ROWS_DEV = 8
CACHE = 512
BATCH = 1024
ATT = 16384
QCOLS = 18432


def draw_lengths(key, part):
    key = jax.random.fold_in(key, 11)
    first, second, third = jax.random.split(key, 3)
    base = jax.random.randint(first, (BATCH,), 1, CACHE + 1)
    factor = jax.random.randint(second, (BATCH // ROWS_DEV,), 1, 5)
    factor = jnp.repeat(factor, ROWS_DEV)
    lengths = jnp.maximum(base // factor, 1)
    chosen = jax.random.randint(third, (), 0, BATCH)
    return jnp.where(jnp.arange(BATCH) == chosen, CACHE, lengths).astype(jnp.int32)


def draw_k_cache(key, part):
    key = jax.random.fold_in(key, 5)
    first = jax.random.fold_in(key, 0)
    values = jax.random.truncated_normal(first, -6.0, 6.0, (BATCH, CACHE, KVH * HD), jnp.float32)
    return values.astype(jnp.bfloat16)


def steps_of(stream_key, shape, cuts, least, largest):
    loudness = 1.0
    for axis_at, parts in cuts:
        draws = jax.random.uniform(jax.random.fold_in(jax.random.fold_in(stream_key, 6), axis_at), (parts,), jnp.float32, least / len(cuts), largest / len(cuts))
        loudness = loudness * jnp.repeat(jnp.exp(draws), shape[axis_at] // parts).reshape((-1,) + (1,) * (len(shape) - 1 - axis_at))
    return loudness


def bell_draw(stream_key, shape, scale, limit, cuts=(), kind=jnp.bfloat16):
    result = scale * jax.random.normal(stream_key, shape, jnp.float32)
    if cuts:
        result = result * steps_of(stream_key, shape, cuts, -0.22, 0.18)
    return jnp.clip(result, -limit, limit).astype(kind)


def setup_inputs(seed: int = 0) -> dict:
    streams_of = jax.random.split(jax.random.key(seed), 8)
    return {
        "hidden_in": bell_draw(streams_of[0], (BATCH, D), 1.0, 6.0, ((0, 128),)),
        "norm_gain": jnp.clip(1.0 + 0.18 * jax.random.normal(streams_of[1], (D,), jnp.float32), 0.1, 1.9),
        "w_qkv": bell_draw(streams_of[2], (D, QCOLS), D ** -0.5, 0.046875, ((0, 4), (1, 32))),
        "k_cache": draw_k_cache(jax.random.fold_in(streams_of[7], 71), 0),
        "v_cache": bell_draw(streams_of[4], (BATCH, CACHE, KVH * HD), 1.0, 6.0, ((0, 128),)),
        "lengths": draw_lengths(jax.random.fold_in(streams_of[7], 71), 0),
        "w_out": bell_draw(streams_of[6], (ATT, D), (ATT // 64) ** -0.5, 0.375, ((0, 4), (1, 32))),
    }


eps = 1e-05
theta = 500000.0

def rotate(values, position, head_size):
    half = head_size // 2
    index = jnp.arange(half, dtype=jnp.float32)
    freqs = theta ** (-2.0 * index / head_size)
    angle = position[:, None, None] * freqs[None, None, :]
    cosine = jnp.cos(angle)
    sine = jnp.sin(angle)
    first = values[..., :half]
    second = values[..., half:]
    return jnp.concatenate([first * cosine - second * sine, second * cosine + first * sine], axis=-1)

def attend_rows(qkv, k_cache, v_cache, lengths):
    rows = qkv.shape[0]
    span = k_cache.shape[1]
    share = HQ // KVH
    query = qkv[:, :HQ * HD].reshape(rows, HQ, HD).astype(jnp.float32)
    key_new = qkv[:, HQ * HD:(HQ + KVH) * HD].reshape(rows, KVH, HD).astype(jnp.float32)
    value_new = qkv[:, (HQ + KVH) * HD:].reshape(rows, KVH, HD).astype(jnp.float32)
    position = lengths.astype(jnp.float32)
    query = rotate(query, position, HD).astype(jnp.bfloat16).astype(jnp.float32)
    key_new = rotate(key_new, position, HD).astype(jnp.bfloat16).astype(jnp.float32)
    grouped = query.reshape(rows, KVH, share, HD)
    keys = k_cache.reshape(rows, span, KVH, HD).astype(jnp.float32)
    values = v_cache.reshape(rows, span, KVH, HD).astype(jnp.float32)
    scale = 1.0 / math.sqrt(HD)
    scores = jnp.einsum('rgsd,rtgd->rgst', grouped, keys) * scale
    fresh = jnp.einsum('rgsd,rgd->rgs', grouped, key_new) * scale
    valid = jnp.arange(span, dtype=jnp.int32)[None, :] < lengths[:, None]
    scores = jnp.where(valid[:, None, None, :], scores, -jnp.inf)
    top = jnp.maximum(lax.optimization_barrier(jnp.max(scores, axis=-1)), fresh)
    probs = jnp.exp(scores - top[..., None])
    pnew = jnp.exp(fresh - top)
    total = lax.optimization_barrier(jnp.sum(probs, axis=-1)) + pnew
    weights = (probs / total[..., None]).astype(jnp.bfloat16).astype(jnp.float32)
    wnew = (pnew / total).astype(jnp.bfloat16).astype(jnp.float32)
    mixed = jnp.einsum('rgst,rtgd->rgsd', weights, values) + wnew[..., None] * value_new[:, :, None, :]
    return mixed.reshape(rows, HQ * HD).astype(jnp.bfloat16)

def reference(hidden_in, norm_gain, w_qkv, k_cache, v_cache, lengths, w_out):
    widened = hidden_in.astype(jnp.float32)
    normed = (widened * lax.rsqrt(lax.optimization_barrier(jnp.mean(widened * widened, axis=-1, keepdims=True)) + eps) * norm_gain).astype(jnp.bfloat16)
    qkv = jnp.dot(normed, w_qkv, preferred_element_type=jnp.float32).astype(jnp.bfloat16)
    blocks = BATCH // ROWS_DEV
    pieces = (qkv.reshape(blocks, ROWS_DEV, QCOLS), k_cache.reshape(blocks, ROWS_DEV, CACHE, KVH * HD), v_cache.reshape(blocks, ROWS_DEV, CACHE, KVH * HD), lengths.reshape(blocks, ROWS_DEV))
    attended = lax.map(lambda p: attend_rows(p[0], p[1], p[2], p[3]), pieces).reshape(BATCH, HQ * HD)
    return jnp.dot(attended, w_out, preferred_element_type=jnp.float32).astype(jnp.bfloat16)
```

```python
import math

import jax
import jax.numpy as jnp
from jax import lax
from jax.sharding import PartitionSpec as P

HQ = 128
KVH = 8
HD = 128


eps = 1e-05
theta = 500000.0


def rotate(values, position, head_size):
    half = head_size // 2
    index = jnp.arange(half, dtype=jnp.float32)
    freqs = theta ** (-2.0 * index / head_size)
    angle = position[:, None, None] * freqs[None, None, :]
    cosine = jnp.cos(angle)
    sine = jnp.sin(angle)
    first = values[..., :half]
    second = values[..., half:]
    return jnp.concatenate(
        [first * cosine - second * sine, second * cosine + first * sine], axis=-1
    )


def normalize(scores, fresh):
    top = jnp.maximum(jnp.max(scores, axis=-1), fresh)
    probs = jnp.exp(scores - top[..., None])
    pnew = jnp.exp(fresh - top)
    total = jnp.sum(probs, axis=-1) + pnew
    return ((probs / total[..., None]).astype(jnp.bfloat16), (pnew / total).astype(jnp.bfloat16))


def attend_local(owned, k_cache, v_cache, lengths):
    rows = owned.shape[0]
    span = k_cache.shape[1]
    share = HQ // KVH
    query = owned[:, : HQ * HD].reshape(rows, HQ, HD).astype(jnp.float32)
    key_new = owned[:, HQ * HD : (HQ + KVH) * HD].reshape(rows, KVH, HD).astype(jnp.float32)
    value_new = owned[:, (HQ + KVH) * HD :].reshape(rows, KVH, HD).astype(jnp.float32)
    position = lengths.astype(jnp.float32)
    grouped = rotate(query, position, HD).astype(jnp.bfloat16).reshape(rows, KVH, share, HD)
    key_new = rotate(key_new, position, HD).astype(jnp.bfloat16)
    keys = k_cache.reshape(rows, span, KVH, HD)
    values = v_cache.reshape(rows, span, KVH, HD)
    scale = 1.0 / math.sqrt(HD)
    fresh = (
        jnp.einsum("rgsd,rgd->rgs", grouped, key_new, preferred_element_type=jnp.float32) * scale
    )
    scores = (
        jnp.einsum("rgsd,rtgd->rgst", grouped, keys, preferred_element_type=jnp.float32) * scale
    )
    valid = jnp.arange(span, dtype=jnp.int32)[None, :] < lengths[:, None]
    scores = jnp.where(valid[:, None, None, :], scores, -jnp.inf)
    weights, wnew = normalize(scores, fresh)
    mixed = jnp.einsum("rgst,rtgd->rgsd", weights, values, preferred_element_type=jnp.float32)
    mixed = mixed + wnew.astype(jnp.float32)[..., None] * value_new[:, :, None, :]
    return mixed.reshape(rows, HQ * HD).astype(jnp.bfloat16)


def gather_rows(rows):
    blocks = rows.reshape(rows.shape[0], 4, -1).transpose(1, 0, 2)
    spread = lax.all_to_all(blocks, "gy", split_axis=0, concat_axis=0, tiled=True)
    return lax.all_gather(spread.reshape(32, -1), "gx", axis=0, tiled=True)


def on_device(hidden_in, norm_gain, w_qkv, k_cache, v_cache, lengths, w_out):
    widened = hidden_in.astype(jnp.float32)
    normed = (
        widened * lax.rsqrt(jnp.mean(widened * widened, axis=-1, keepdims=True) + eps) * norm_gain
    ).astype(jnp.bfloat16)
    picked = gather_rows(normed)
    partial_qkv = lax.psum_scatter(
        jnp.dot(picked, w_qkv, preferred_element_type=jnp.float32).reshape(32, 4, 8, -1)
        .transpose(1, 0, 2, 3)
        .reshape(1024, -1),
        "gy",
        scatter_dimension=0,
        tiled=True,
    )
    owned = lax.all_to_all(
        partial_qkv.astype(jnp.bfloat16), "gx", split_axis=0, concat_axis=1, tiled=True
    )
    attended = attend_local(owned, k_cache, v_cache, lengths)
    picked = gather_rows(attended)
    partial_out = lax.psum_scatter(
        jnp.dot(picked, w_out, preferred_element_type=jnp.float32)
        .astype(jnp.bfloat16)
        .reshape(32, 4, 8, -1)
        .transpose(1, 0, 2, 3)
        .reshape(1024, -1),
        "gy",
        scatter_dimension=0,
        tiled=True,
    )
    return lax.all_to_all(partial_out, "gx", split_axis=0, concat_axis=1, tiled=True)


def solution(mesh):
    return jax.shard_map(
        on_device,
        mesh=mesh,
        in_specs=(
            P(("gx", "gy"), None),
            P(),
            P("gy", "gx"),
            P(("gx", "gy"), None, None),
            P(("gx", "gy"), None, None),
            P(("gx", "gy")),
            P("gy", "gx"),
        ),
        out_specs=P(("gx", "gy"), None),
        check_vma=False,
    )
```

```python
import functools
import math

import jax
import jax.numpy as jnp
from jax import lax
from jax.experimental import pallas as pl
from jax.experimental.pallas import tpu as pltpu
from jax.sharding import PartitionSpec as P

HQ = 128
KVH = 8
HD = 128
DEPTH = 4096
QWIDE = 640

eps = 1e-05
theta = 500000.0

UNITS = (
    ((0, 0), (0, 3), (0, 1), (0, 2)),
    ((1, 0), (3, 0), (1, 3), (3, 3)),
    ((1, 1), (3, 1), (1, 2), (3, 2)),
    ((2, 0), (2, 3), (2, 1), (2, 2)),
)
PLACE = {ur: (w, i) for w, unit in enumerate(UNITS) for i, ur in enumerate(unit)}


def remote(src, dst, send, recv, device):
    return pltpu.make_async_remote_copy(
        src_ref=src,
        dst_ref=dst,
        send_sem=send,
        recv_sem=recv,
        device_id=device,
        device_id_type=pl.DeviceIdType.MESH,
    )


class Here:
    def __init__(self):
        gx = lax.axis_index("gx")
        self.gx = gx
        self.z = lax.axis_index("gy")
        self.y = gx // 8
        self.x = (gx // 2) % 4
        self.c = gx % 2

    def device(self, dy=0, dx=0, dc=0, dz=0):
        y = (self.y + dy) % 4
        x = (self.x + dx) % 4
        c = (self.c + dc) % 2
        return ((y * 4 + x) * 2 + c, (self.z + dz) % 4)

    def greet(self):
        barrier = pltpu.get_barrier_semaphore()
        for dy in range(4):
            for dx in range(4):
                for dc in range(2):
                    if dy or dx or dc:
                        pl.semaphore_signal(
                            barrier,
                            inc=1,
                            device_id=self.device(dy, dx, dc),
                            device_id_type=pl.DeviceIdType.MESH,
                        )
        for dz in range(1, 4):
            pl.semaphore_signal(
                barrier,
                inc=1,
                device_id=self.device(dz=dz),
                device_id_type=pl.DeviceIdType.MESH,
            )

    def greeted(self):
        pl.semaphore_wait(pltpu.get_barrier_semaphore(), 34)


class Projection:
    def __init__(self, here, refs, weight, wide, transposed):
        self.here = here
        self.weight = weight
        self.wide = wide
        self.transposed = transposed
        (
            self.mine,
            self.spread,
            self.rows,
            self.partial,
            self.relay,
            self.last,
            self.ready,
            self.owned,
            self.zsem,
            self.gsem,
            self.csem,
            self.rsem,
            self.osem,
        ) = refs
        self.sent = []

    @staticmethod
    def scratch(wide, kind):
        return [
            pltpu.VMEM((4, 8, DEPTH), jnp.bfloat16),
            pltpu.VMEM((4, 8, DEPTH), jnp.bfloat16),
            pltpu.VMEM((1024, DEPTH), jnp.bfloat16),
            pltpu.VMEM((4, 4, 64, wide), kind),
            pltpu.VMEM((4, 2, 32, wide), kind),
            pltpu.VMEM((4, 2, 64, wide), kind),
            pltpu.VMEM((4, 8, 8, wide), jnp.bfloat16),
            pltpu.VMEM((32, 8, wide), jnp.bfloat16),
            pltpu.SemaphoreType.DMA((2, 4)),
            pltpu.SemaphoreType.DMA((2, 128)),
            pltpu.SemaphoreType.DMA((2, 32)),
            pltpu.SemaphoreType.DMA((2, 16)),
            pltpu.SemaphoreType.DMA((2, 32)),
        ]

    def push(self, *args):
        copy = remote(*args)
        copy.start()
        self.sent.append(copy)

    def exchange(self):
        z = self.here.z
        for dz in (1, 3, 2):
            to = (z + dz) % 4
            self.push(
                self.mine.at[to],
                self.spread.at[z],
                self.zsem.at[0, dz],
                self.zsem.at[1, dz],
                self.here.device(dz=dz),
            )
        self.spread[z] = self.mine[z]

    def exchanged(self):
        z = self.here.z
        for dz in (1, 3, 2):
            slot = self.spread.at[(z + 4 - dz) % 4]
            remote(
                slot, slot, self.zsem.at[0, dz], self.zsem.at[1, dz], self.here.device(dz=1)
            ).wait_recv()
        for part in range(2):
            both = jnp.concatenate([self.spread[2 * part], self.spread[2 * part + 1]], axis=0)
            self.rows[pl.ds(self.start_of(part, 0, 0, 0), 16), :] = both

    def start_of(self, part, u, r, core):
        w, i = PLACE[(u, r)]
        return w * 256 + part * 128 + (i * 2 + core) * 16

    def slot(self, part, u, r, core, half=None):
        columns = pl.ds(0, DEPTH) if half is None else pl.ds(half * (DEPTH // 2), DEPTH // 2)
        return self.rows.at[pl.ds(self.start_of(part, u, r, core), 16), columns]

    def gather_sem(self, side, part, u, r, half):
        return self.gsem.at[side, ((part * 4 + u) * 4 + r) * 2 + (half or 0)]

    def along(self, part, first, step):
        if first == (part == 0):
            return self.here.device(dx=step)
        return self.here.device(dy=step)

    def hop(self, part, u, r, first, step, half=None):
        nu, nr = (u, (r - step) % 4) if first else ((u - step) % 4, r)
        self.push(
            self.slot(part, u, r, 0, half),
            self.slot(part, nu, nr, 0, half),
            self.gather_sem(0, part, nu, nr, half),
            self.gather_sem(1, part, nu, nr, half),
            self.along(part, first, step),
        )

    def to_sibling(self, part, u, r):
        k = (part * 4 + u) * 4 + r
        self.push(
            self.slot(part, u, r, 0),
            self.slot(part, u, r, 1),
            self.csem.at[0, k],
            self.csem.at[1, k],
            self.here.device(dc=1),
        )

    def arrived(self, part, u, r):
        halves = (0, 1) if (u == 2 or (u == 0 and r == 2)) else (None,)
        for half in halves:
            slot = self.slot(part, u, r, 0, half)
            remote(
                slot,
                slot,
                self.gather_sem(0, part, u, r, half),
                self.gather_sem(1, part, u, r, half),
                self.here.device(dc=1),
            ).wait_recv()

    def sibling_arrived(self, part, u, r):
        k = (part * 4 + u) * 4 + r
        slot = self.slot(part, u, r, 1)
        remote(
            slot, slot, self.csem.at[0, k], self.csem.at[1, k], self.here.device(dc=1)
        ).wait_recv()

    def second(self, part, r):
        self.hop(part, 0, r, False, 1)
        self.hop(part, 0, r, False, -1)
        self.to_sibling(part, 0, r)

    def first_ring(self):
        for part in range(2):
            self.hop(part, 0, 0, True, 1)
            self.hop(part, 0, 0, True, -1)
        for part in range(2):
            self.second(part, 0)
        for r, step in ((3, 1), (1, -1)):
            for part in range(2):
                self.arrived(part, 0, r)
                self.hop(part, 0, r, True, step, 0 if step == 1 else 1)
                self.second(part, r)
        for part in range(2):
            self.arrived(part, 0, 2)
            self.second(part, 2)

    def second_ring(self, r):
        for u, step in ((3, 1), (1, -1)):
            for part in range(2):
                self.arrived(part, u, r)
                self.hop(part, u, r, False, step, 0 if step == 1 else 1)
                self.to_sibling(part, u, r)

    def last_ring(self):
        for r in (0, 3, 1, 2):
            for part in range(2):
                self.arrived(part, 2, r)
                self.to_sibling(part, 2, r)

    def dots(self, w):
        for u, r in UNITS[w]:
            for part in range(2):
                self.sibling_arrived(part, u, r)

        def tile(start, width):
            lhs = self.rows[pl.ds(w * 256, 256), :]
            if self.transposed:
                out = lax.dot_general(
                    lhs,
                    self.weight[pl.ds(start, width), :],
                    (((1,), (1,)), ((), ())),
                    preferred_element_type=jnp.float32,
                )
            else:
                out = jnp.dot(
                    lhs,
                    self.weight[:, pl.ds(start, width)],
                    preferred_element_type=jnp.float32,
                )
            out = out.reshape(2, 8, 2, 8, width)
            for d in range(4):
                self.partial[w, d, :, pl.ds(start, width)] = (
                    out[d // 2, :, d % 2].reshape(64, width).astype(self.partial.dtype)
                )

        @pl.loop(0, self.wide // 256)
        def _(n):
            tile(pl.multiple_of(n * 256, 256), 256)

        if self.wide % 256:
            tile(self.wide // 256 * 256, self.wide % 256)

    def ring_copy(self, src, dst, k, dz):
        self.push(src, dst, self.rsem.at[0, k], self.rsem.at[1, k], self.here.device(dz=dz))

    def ring_wait(self, dst, k):
        remote(
            dst, dst, self.rsem.at[0, k], self.rsem.at[1, k], self.here.device(dz=1)
        ).wait_recv()

    def relay_out(self, w):
        far = (self.here.z + 2) % 4
        self.ring_copy(self.partial.at[w, far, pl.ds(0, 32)], self.relay.at[w, 0], w * 4, 1)
        self.ring_copy(self.partial.at[w, far, pl.ds(32, 32)], self.relay.at[w, 1], w * 4 + 1, -1)

    def neighbours_out(self, w):
        for side, dz in ((0, 1), (1, -1)):
            to = (self.here.z + dz) % 4
            half = pl.ds(32 * side, 32)
            self.ring_wait(self.relay.at[w, side], w * 4 + side)
            total = self.partial[w, to, half, :].astype(jnp.float32) + self.relay[w, side].astype(
                jnp.float32
            )
            self.partial[w, to, half, :] = total.astype(self.partial.dtype)
            self.ring_copy(self.partial.at[w, to], self.last.at[w, side], w * 4 + 2 + side, dz)

    def owners_out(self, w):
        here = self.here
        total = self.partial[w, here.z].astype(jnp.float32)
        for side in range(2):
            self.ring_wait(self.last.at[w, side], w * 4 + 2 + side)
            total = total + self.last[w, side].astype(jnp.float32)
        self.ready[w] = total.reshape(8, 8, self.wide).astype(jnp.bfloat16)
        for i, (u, r) in enumerate(UNITS[w]):
            for core in range(2):
                j = i * 2 + core
                if w == 0 and j == 0:
                    self.owned[here.gx] = self.ready[0, 0]
                    continue
                self.push(
                    self.ready.at[w, j],
                    self.owned.at[here.gx],
                    self.osem.at[0, w * 8 + j],
                    self.osem.at[1, w * 8 + j],
                    self.owner(u, r, core),
                )

    def owner(self, u, r, core):
        first = self.here.z < 2
        dy = jnp.where(first, u, r)
        dx = jnp.where(first, r, u)
        return self.here.device(dy, dx, core)

    def owners_in(self):
        for w in range(4):
            for i, (u, r) in enumerate(UNITS[w]):
                for core in range(2):
                    j = i * 2 + core
                    if w == 0 and j == 0:
                        continue
                    source, _ = self.owner(4 - u, 4 - r, core)
                    slot = self.owned.at[source]
                    remote(
                        slot,
                        slot,
                        self.osem.at[0, w * 8 + j],
                        self.osem.at[1, w * 8 + j],
                        self.here.device(dc=1),
                    ).wait_recv()

    def run(self, weight_in):
        self.exchanged()
        self.first_ring()
        weight_in()
        self.dots(0)
        self.relay_out(0)
        self.second_ring(0)
        self.second_ring(3)
        self.neighbours_out(0)
        self.dots(1)
        self.relay_out(1)
        self.second_ring(1)
        self.second_ring(2)
        self.neighbours_out(1)
        self.dots(2)
        self.relay_out(2)
        self.owners_out(0)
        self.last_ring()
        self.neighbours_out(2)
        self.dots(3)
        self.relay_out(3)
        self.owners_out(1)
        self.neighbours_out(3)
        self.owners_out(2)
        self.owners_out(3)
        self.owners_in()

    def finish(self):
        for copy in self.sent:
            copy.wait_send()


def project_in(hidden, gain, w_t, out, weight, wsem, *refs):
    here = Here()
    here.greet()
    load = pltpu.make_async_copy(
        w_t, weight.at[pl.ds(pl.multiple_of(here.c * 64, 64), 576), :], wsem
    )
    load.start()
    weight[pl.ds(pl.multiple_of((1 - here.c) * 576, 64), 64), :] = jnp.zeros(
        (64, DEPTH), jnp.bfloat16
    )
    step = Projection(here, refs, weight, QWIDE, True)
    widened = hidden[...].astype(jnp.float32)
    scale = lax.rsqrt(jnp.mean(widened * widened, axis=-1, keepdims=True) + eps)
    for z in range(4):
        columns = pl.ds(z * DEPTH, DEPTH)
        step.mine[z] = (hidden[:, columns].astype(jnp.float32) * scale * gain[:, columns]).astype(
            jnp.bfloat16
        )
    here.greeted()
    step.exchange()
    step.run(load.wait)
    out[...] = step.owned[...]
    step.finish()


def project_out(attended, w, out, weight, wsem, *refs):
    here = Here()
    here.greet()
    load = pltpu.make_async_copy(w, weight, wsem)
    load.start()
    step = Projection(here, refs, weight, 512, False)
    for z in range(4):
        step.mine[z] = attended[:, pl.ds(z * DEPTH, DEPTH)]
    here.greeted()
    step.exchange()
    step.run(load.wait)
    for g in range(32):
        out[:, pl.ds(g * 512, 512)] = step.owned[g]
    step.finish()


def vmem():
    return pl.BlockSpec(memory_space=pltpu.VMEM)


def hbm():
    return pl.BlockSpec(memory_space=pl.ANY)


def call_in(hidden, gain, w_t):
    return pl.pallas_call(
        project_in,
        out_shape=jax.ShapeDtypeStruct((32, 8, QWIDE), jnp.bfloat16),
        in_specs=[vmem(), vmem(), hbm()],
        out_specs=vmem(),
        scratch_shapes=[pltpu.VMEM((QWIDE, DEPTH), jnp.bfloat16), pltpu.SemaphoreType.DMA]
        + Projection.scratch(QWIDE, jnp.float32),
        compiler_params=pltpu.CompilerParams(
            collective_id=0, has_side_effects=True, vmem_limit_bytes=56 * 1024 * 1024
        ),
        name="project_in",
    )(hidden, gain.reshape(1, -1), w_t)


def call_out(attended, w):
    return pl.pallas_call(
        project_out,
        out_shape=jax.ShapeDtypeStruct((8, 16384), jnp.bfloat16),
        in_specs=[vmem(), hbm()],
        out_specs=vmem(),
        scratch_shapes=[pltpu.VMEM((DEPTH, 512), jnp.bfloat16), pltpu.SemaphoreType.DMA]
        + Projection.scratch(512, jnp.bfloat16),
        compiler_params=pltpu.CompilerParams(
            collective_id=1, has_side_effects=True, vmem_limit_bytes=56 * 1024 * 1024
        ),
        name="project_out",
    )(attended, w)


def rotate(values, position, head_size):
    half = head_size // 2
    index = jnp.arange(half, dtype=jnp.float32)
    freqs = theta ** (-2.0 * index / head_size)
    angle = position[:, None, None] * freqs[None, None, :]
    cosine = jnp.cos(angle)
    sine = jnp.sin(angle)
    first = values[..., :half]
    second = values[..., half:]
    return jnp.concatenate(
        [first * cosine - second * sine, second * cosine + first * sine], axis=-1
    )


def normalize(scores, fresh):
    top = jnp.maximum(jnp.max(scores, axis=-1), fresh)
    probs = jnp.exp(scores - top[..., None])
    pnew = jnp.exp(fresh - top)
    total = jnp.sum(probs, axis=-1) + pnew
    return ((probs / total[..., None]).astype(jnp.bfloat16), (pnew / total).astype(jnp.bfloat16))


def attend_local(owned, k_cache, v_cache, lengths):
    rows = owned.shape[0]
    span = k_cache.shape[1]
    share = HQ // KVH
    query = owned[:, : HQ * HD].reshape(rows, HQ, HD).astype(jnp.float32)
    key_new = owned[:, HQ * HD : (HQ + KVH) * HD].reshape(rows, KVH, HD).astype(jnp.float32)
    value_new = owned[:, (HQ + KVH) * HD :].reshape(rows, KVH, HD).astype(jnp.float32)
    position = lengths.astype(jnp.float32)
    grouped = rotate(query, position, HD).astype(jnp.bfloat16).reshape(rows, KVH, share, HD)
    key_new = rotate(key_new, position, HD).astype(jnp.bfloat16)
    keys = k_cache.reshape(rows, span, KVH, HD)
    values = v_cache.reshape(rows, span, KVH, HD)
    scale = 1.0 / math.sqrt(HD)
    fresh = (
        jnp.einsum("rgsd,rgd->rgs", grouped, key_new, preferred_element_type=jnp.float32) * scale
    )
    scores = (
        jnp.einsum("rgsd,rtgd->rgst", grouped, keys, preferred_element_type=jnp.float32) * scale
    )
    valid = jnp.arange(span, dtype=jnp.int32)[None, :] < lengths[:, None]
    scores = jnp.where(valid[:, None, None, :], scores, -jnp.inf)
    weights, wnew = normalize(scores, fresh)
    mixed = jnp.einsum("rgst,rtgd->rgsd", weights, values, preferred_element_type=jnp.float32)
    mixed = mixed + wnew.astype(jnp.float32)[..., None] * value_new[:, :, None, :]
    return mixed.reshape(rows, HQ * HD).astype(jnp.bfloat16)


def on_device(hidden_in, norm_gain, w_qkv, k_cache, v_cache, lengths, w_out):
    blocks = call_in(hidden_in, norm_gain, w_qkv.T)
    pairs = blocks.reshape(16, 2, 8, QWIDE)
    joined = jnp.concatenate([pairs[:, 0, :, :576], pairs[:, 1, :, 64:]], axis=-1)
    owned = joined.transpose(1, 0, 2).reshape(8, 18432)
    attended = attend_local(owned, k_cache, v_cache, lengths)
    return call_out(attended, w_out)


def solution(mesh):
    return jax.shard_map(
        on_device,
        mesh=mesh,
        in_specs=(
            P(("gx", "gy"), None),
            P(),
            P("gy", "gx"),
            P(("gx", "gy"), None, None),
            P(("gx", "gy"), None, None),
            P(("gx", "gy")),
            P("gy", "gx"),
        ),
        out_specs=P(("gx", "gy"), None),
        check_vma=False,
    )
```

```python
import math

import jax
import jax.numpy as jnp
from jax import lax
from jax.experimental import pallas as pl
from jax.experimental.pallas import tpu as pltpu
from jax.sharding import PartitionSpec as P

HQ = 128
KVH = 8
HD = 128
ROWS = 8
CACHE = 512
DEPTH = 4096
QWIDE = 640

eps = 1e-05
theta = 500000.0

UNITS = (
    ((0, 0), (0, 3), (0, 1), (0, 2)),
    ((1, 0), (3, 0), (1, 3), (3, 3)),
    ((1, 1), (3, 1), (1, 2), (3, 2)),
    ((2, 0), (2, 3), (2, 1), (2, 2)),
)
PLACE = {ur: (w, i) for w, unit in enumerate(UNITS) for i, ur in enumerate(unit)}


def remote(src, dst, send, recv, device):
    return pltpu.make_async_remote_copy(
        src_ref=src,
        dst_ref=dst,
        send_sem=send,
        recv_sem=recv,
        device_id=device,
        device_id_type=pl.DeviceIdType.MESH,
    )


class Here:
    def __init__(self):
        gx = lax.axis_index("gx")
        self.gx = gx
        self.z = lax.axis_index("gy")
        self.y = gx // 8
        self.x = (gx // 2) % 4
        self.c = gx % 2

    def device(self, dy=0, dx=0, dc=0, dz=0):
        y = (self.y + dy) % 4
        x = (self.x + dx) % 4
        c = (self.c + dc) % 2
        return ((y * 4 + x) * 2 + c, (self.z + dz) % 4)

    def greet(self):
        barrier = pltpu.get_barrier_semaphore()
        for dy in range(4):
            for dx in range(4):
                for dc in range(2):
                    if dy or dx or dc:
                        pl.semaphore_signal(
                            barrier,
                            inc=1,
                            device_id=self.device(dy, dx, dc),
                            device_id_type=pl.DeviceIdType.MESH,
                        )
        for dz in range(1, 4):
            pl.semaphore_signal(
                barrier,
                inc=1,
                device_id=self.device(dz=dz),
                device_id_type=pl.DeviceIdType.MESH,
            )

    def greeted(self):
        pl.semaphore_wait(pltpu.get_barrier_semaphore(), 34)


class Projection:
    def __init__(self, here, refs, weight, wide, transposed):
        self.here = here
        self.weight = weight
        self.wide = wide
        self.transposed = transposed
        (
            self.mine,
            self.spread,
            self.rows,
            self.partial,
            self.relay,
            self.last,
            self.ready,
            self.owned,
            self.zsem,
            self.gsem,
            self.csem,
            self.rsem,
            self.osem,
        ) = refs
        self.sent = []

    @staticmethod
    def scratch(wide, kind):
        return [
            pltpu.VMEM((4, 8, DEPTH), jnp.bfloat16),
            pltpu.VMEM((4, 8, DEPTH), jnp.bfloat16),
            pltpu.VMEM((1024, DEPTH), jnp.bfloat16),
            pltpu.VMEM((4, 4, 64, wide), kind),
            pltpu.VMEM((4, 2, 32, wide), kind),
            pltpu.VMEM((4, 2, 64, wide), kind),
            pltpu.VMEM((4, 8, 8, wide), jnp.bfloat16),
            pltpu.VMEM((32, 8, wide), jnp.bfloat16),
            pltpu.SemaphoreType.DMA((2, 4)),
            pltpu.SemaphoreType.DMA((2, 128)),
            pltpu.SemaphoreType.DMA((2, 32)),
            pltpu.SemaphoreType.DMA((2, 16)),
            pltpu.SemaphoreType.DMA((2, 32)),
        ]

    def push(self, *args):
        copy = remote(*args)
        copy.start()
        self.sent.append(copy)

    def exchange(self):
        z = self.here.z
        for dz in (1, 3, 2):
            to = (z + dz) % 4
            self.push(
                self.mine.at[to],
                self.spread.at[z],
                self.zsem.at[0, dz],
                self.zsem.at[1, dz],
                self.here.device(dz=dz),
            )
        self.spread[z] = self.mine[z]

    def exchanged(self):
        z = self.here.z
        for dz in (1, 3, 2):
            slot = self.spread.at[(z + 4 - dz) % 4]
            remote(
                slot, slot, self.zsem.at[0, dz], self.zsem.at[1, dz], self.here.device(dz=1)
            ).wait_recv()
        for part in range(2):
            both = jnp.concatenate([self.spread[2 * part], self.spread[2 * part + 1]], axis=0)
            self.rows[pl.ds(self.start_of(part, 0, 0, 0), 16), :] = both

    def start_of(self, part, u, r, core):
        w, i = PLACE[(u, r)]
        return w * 256 + part * 128 + (i * 2 + core) * 16

    def slot(self, part, u, r, core, half=None):
        columns = pl.ds(0, DEPTH) if half is None else pl.ds(half * (DEPTH // 2), DEPTH // 2)
        return self.rows.at[pl.ds(self.start_of(part, u, r, core), 16), columns]

    def gather_sem(self, side, part, u, r, half):
        return self.gsem.at[side, ((part * 4 + u) * 4 + r) * 2 + (half or 0)]

    def along(self, part, first, step):
        if first == (part == 0):
            return self.here.device(dx=step)
        return self.here.device(dy=step)

    def hop(self, part, u, r, first, step, half=None):
        nu, nr = (u, (r - step) % 4) if first else ((u - step) % 4, r)
        self.push(
            self.slot(part, u, r, 0, half),
            self.slot(part, nu, nr, 0, half),
            self.gather_sem(0, part, nu, nr, half),
            self.gather_sem(1, part, nu, nr, half),
            self.along(part, first, step),
        )

    def to_sibling(self, part, u, r):
        k = (part * 4 + u) * 4 + r
        self.push(
            self.slot(part, u, r, 0),
            self.slot(part, u, r, 1),
            self.csem.at[0, k],
            self.csem.at[1, k],
            self.here.device(dc=1),
        )

    def arrived(self, part, u, r):
        halves = (0, 1) if (u == 2 or (u == 0 and r == 2)) else (None,)
        for half in halves:
            slot = self.slot(part, u, r, 0, half)
            remote(
                slot,
                slot,
                self.gather_sem(0, part, u, r, half),
                self.gather_sem(1, part, u, r, half),
                self.here.device(dc=1),
            ).wait_recv()

    def sibling_arrived(self, part, u, r):
        k = (part * 4 + u) * 4 + r
        slot = self.slot(part, u, r, 1)
        remote(
            slot, slot, self.csem.at[0, k], self.csem.at[1, k], self.here.device(dc=1)
        ).wait_recv()

    def second(self, part, r):
        self.hop(part, 0, r, False, 1)
        self.hop(part, 0, r, False, -1)
        self.to_sibling(part, 0, r)

    def first_ring(self):
        for part in range(2):
            self.hop(part, 0, 0, True, 1)
            self.hop(part, 0, 0, True, -1)
        for part in range(2):
            self.second(part, 0)
        for r, step in ((3, 1), (1, -1)):
            for part in range(2):
                self.arrived(part, 0, r)
                self.hop(part, 0, r, True, step, 0 if step == 1 else 1)
                self.second(part, r)
        for part in range(2):
            self.arrived(part, 0, 2)
            self.second(part, 2)

    def second_ring(self, r):
        for u, step in ((3, 1), (1, -1)):
            for part in range(2):
                self.arrived(part, u, r)
                self.hop(part, u, r, False, step, 0 if step == 1 else 1)
                self.to_sibling(part, u, r)

    def last_ring(self):
        for r in (0, 3, 1, 2):
            for part in range(2):
                self.arrived(part, 2, r)
                self.to_sibling(part, 2, r)

    def dots(self, w):
        for u, r in UNITS[w]:
            for part in range(2):
                self.sibling_arrived(part, u, r)

        def tile(start, width):
            lhs = self.rows[pl.ds(w * 256, 256), :]
            if self.transposed:
                out = lax.dot_general(
                    lhs,
                    self.weight[pl.ds(start, width), :],
                    (((1,), (1,)), ((), ())),
                    preferred_element_type=jnp.float32,
                )
            else:
                out = jnp.dot(
                    lhs,
                    self.weight[:, pl.ds(start, width)],
                    preferred_element_type=jnp.float32,
                )
            out = out.reshape(2, 8, 2, 8, width)
            for d in range(4):
                self.partial[w, d, :, pl.ds(start, width)] = (
                    out[d // 2, :, d % 2].reshape(64, width).astype(self.partial.dtype)
                )

        @pl.loop(0, self.wide // 256)
        def _(n):
            tile(pl.multiple_of(n * 256, 256), 256)

        if self.wide % 256:
            tile(self.wide // 256 * 256, self.wide % 256)

    def ring_copy(self, src, dst, k, dz):
        self.push(src, dst, self.rsem.at[0, k], self.rsem.at[1, k], self.here.device(dz=dz))

    def ring_wait(self, dst, k):
        remote(
            dst, dst, self.rsem.at[0, k], self.rsem.at[1, k], self.here.device(dz=1)
        ).wait_recv()

    def relay_out(self, w):
        far = (self.here.z + 2) % 4
        self.ring_copy(self.partial.at[w, far, pl.ds(0, 32)], self.relay.at[w, 0], w * 4, 1)
        self.ring_copy(self.partial.at[w, far, pl.ds(32, 32)], self.relay.at[w, 1], w * 4 + 1, -1)

    def neighbours_out(self, w):
        for side, dz in ((0, 1), (1, -1)):
            to = (self.here.z + dz) % 4
            half = pl.ds(32 * side, 32)
            self.ring_wait(self.relay.at[w, side], w * 4 + side)
            total = self.partial[w, to, half, :].astype(jnp.float32) + self.relay[w, side].astype(
                jnp.float32
            )
            self.partial[w, to, half, :] = total.astype(self.partial.dtype)
            self.ring_copy(self.partial.at[w, to], self.last.at[w, side], w * 4 + 2 + side, dz)

    def owners_out(self, w):
        here = self.here
        total = self.partial[w, here.z].astype(jnp.float32)
        for side in range(2):
            self.ring_wait(self.last.at[w, side], w * 4 + 2 + side)
            total = total + self.last[w, side].astype(jnp.float32)
        self.ready[w] = total.reshape(8, 8, self.wide).astype(jnp.bfloat16)
        for i, (u, r) in enumerate(UNITS[w]):
            for core in range(2):
                j = i * 2 + core
                if w == 0 and j == 0:
                    self.owned[here.gx] = self.ready[0, 0]
                    continue
                self.push(
                    self.ready.at[w, j],
                    self.owned.at[here.gx],
                    self.osem.at[0, w * 8 + j],
                    self.osem.at[1, w * 8 + j],
                    self.owner(u, r, core),
                )

    def owner(self, u, r, core):
        first = self.here.z < 2
        dy = jnp.where(first, u, r)
        dx = jnp.where(first, r, u)
        return self.here.device(dy, dx, core)

    def owners_in(self):
        for w in range(4):
            for i, (u, r) in enumerate(UNITS[w]):
                for core in range(2):
                    j = i * 2 + core
                    if w == 0 and j == 0:
                        continue
                    source, _ = self.owner(4 - u, 4 - r, core)
                    slot = self.owned.at[source]
                    remote(
                        slot,
                        slot,
                        self.osem.at[0, w * 8 + j],
                        self.osem.at[1, w * 8 + j],
                        self.here.device(dc=1),
                    ).wait_recv()

    def run(self, weight_in):
        self.exchanged()
        self.first_ring()
        weight_in()
        self.dots(0)
        self.relay_out(0)
        self.second_ring(0)
        self.second_ring(3)
        self.neighbours_out(0)
        self.dots(1)
        self.relay_out(1)
        self.second_ring(1)
        self.second_ring(2)
        self.neighbours_out(1)
        self.dots(2)
        self.relay_out(2)
        self.owners_out(0)
        self.last_ring()
        self.neighbours_out(2)
        self.dots(3)
        self.relay_out(3)
        self.owners_out(1)
        self.neighbours_out(3)
        self.owners_out(2)
        self.owners_out(3)
        self.owners_in()

    def finish(self):
        for copy in self.sent:
            copy.wait_send()


def normalized(step, hidden, gain):
    widened = hidden[...].astype(jnp.float32)
    scale = lax.rsqrt(jnp.mean(widened * widened, axis=-1, keepdims=True) + eps)
    for z in range(4):
        columns = pl.ds(z * DEPTH, DEPTH)
        step.mine[z] = (hidden[:, columns].astype(jnp.float32) * scale * gain[:, columns]).astype(
            jnp.bfloat16
        )


def turn(lengths, freqs, turns):
    row = lax.broadcasted_iota(jnp.int32, (ROWS, HD), 0)
    lane = lax.broadcasted_iota(jnp.int32, (ROWS, HD), 1)
    position = jnp.zeros((ROWS, HD), jnp.float32)
    for r in range(ROWS):
        position = jnp.where(row == r, lengths[r].astype(jnp.float32), position)
    angle = position * freqs[...]
    turns[0] = jnp.cos(angle)
    turns[1] = jnp.where(lane < HD // 2, -jnp.sin(angle), jnp.sin(angle))


def heads(owned, turns, qkv):
    lane = lax.broadcasted_iota(jnp.int32, (ROWS, HD), 1)
    for pair in range(16):
        even = owned[2 * pair].astype(jnp.float32)
        odd = owned[2 * pair + 1].astype(jnp.float32)
        for t in range(9):
            if t < 4:
                head = even[:, t * HD : (t + 1) * HD]
            elif t > 4:
                head = odd[:, (t - 4) * HD : (t - 3) * HD]
            else:
                head = jnp.where(lane < HD // 2, even[:, 4 * HD :], odd[:, :HD])
            h = pair * 9 + t
            if h < HQ + KVH:
                head = head * turns[0] + pltpu.roll(head, HD // 2, 1) * turns[1]
                head = head.astype(jnp.bfloat16).astype(jnp.float32)
            qkv[pl.ds(h * ROWS, ROWS), :] = head


def attend(lengths, keys, values, qkv, mixed, out):
    share = HQ // KVH
    scale = 1.0 / math.sqrt(HD)

    @pl.loop(0, ROWS)
    def _(r):
        valid = lax.broadcasted_iota(jnp.int32, (share, CACHE), 1) < lengths[r]
        for g in range(KVH):
            columns = pl.ds(g * HD, HD)
            span = pl.ds(g * share * ROWS + r, share, stride=ROWS)
            query = qkv[span, :]
            key_new = qkv[pl.ds((HQ + g) * ROWS + r, 1), :]
            value_new = qkv[pl.ds((HQ + KVH + g) * ROWS + r, 1), :]
            fresh = jnp.sum(query * key_new, axis=1, keepdims=True) * scale
            scores = (
                lax.dot_general(
                    query.astype(jnp.bfloat16),
                    keys[r, :, columns],
                    (((1,), (1,)), ((), ())),
                    preferred_element_type=jnp.float32,
                )
                * scale
            )
            scores = jnp.where(valid, scores, -jnp.inf)
            top = jnp.maximum(jnp.max(scores, axis=1, keepdims=True), fresh)
            probs = jnp.exp(scores - top)
            pnew = jnp.exp(fresh - top)
            total = jnp.sum(probs, axis=1, keepdims=True) + pnew
            weights = (probs / total).astype(jnp.bfloat16)
            wnew = (pnew / total).astype(jnp.bfloat16).astype(jnp.float32)
            mixed[span, :] = (
                jnp.dot(weights, values[r, :, columns], preferred_element_type=jnp.float32)
                + wnew * value_new
            )

    for h in range(HQ):
        out[h // 32, :, pl.ds(h % 32 * HD, HD)] = mixed[pl.ds(h * ROWS, ROWS), :].astype(
            jnp.bfloat16
        )


def layer(
    lengths,
    hidden,
    gain,
    freqs,
    w_qkv,
    k_cache,
    v_cache,
    w_out,
    out,
    weight_in,
    keys,
    values,
    weight_out,
    turns,
    qkv,
    mixed,
    loads,
    *refs,
):
    here = Here()
    here.greet()
    count = len(refs) // 2
    first = Projection(here, refs[:count], weight_in, QWIDE, True)
    second = Projection(here, refs[count:], weight_out, 512, False)
    fetch = [
        pltpu.make_async_copy(
            w_qkv, weight_in.at[pl.ds(pl.multiple_of(here.c * 64, 64), 576), :], loads.at[0]
        ),
        pltpu.make_async_copy(k_cache, keys, loads.at[1]),
        pltpu.make_async_copy(v_cache, values, loads.at[2]),
        pltpu.make_async_copy(w_out, weight_out, loads.at[3]),
    ]
    for copy in fetch:
        copy.start()
    weight_in[pl.ds(pl.multiple_of((1 - here.c) * 576, 64), 64), :] = jnp.zeros(
        (64, DEPTH), jnp.bfloat16
    )
    normalized(first, hidden, gain)
    here.greeted()
    first.exchange()
    turn(lengths, freqs, turns)
    first.run(fetch[0].wait)
    heads(first.owned, turns, qkv)
    fetch[1].wait()
    fetch[2].wait()
    attend(lengths, keys, values, qkv, mixed, second.mine)
    second.exchange()
    second.run(fetch[3].wait)
    out[...] = second.owned[...]
    first.finish()
    second.finish()


def on_device(hidden_in, norm_gain, w_qkv, k_cache, v_cache, lengths, w_out):
    half = jnp.arange(HD // 2, dtype=jnp.float32)
    freqs = theta ** (-2.0 * half / HD)
    freqs = jnp.concatenate([freqs, freqs]).reshape(1, HD)
    vmem = pl.BlockSpec(memory_space=pltpu.VMEM)
    hbm = pl.BlockSpec(memory_space=pl.ANY)
    blocks = pl.pallas_call(
        layer,
        out_shape=jax.ShapeDtypeStruct((32, ROWS, 512), jnp.bfloat16),
        in_specs=[pl.BlockSpec(memory_space=pltpu.SMEM), vmem, vmem, vmem, hbm, hbm, hbm, hbm],
        out_specs=vmem,
        scratch_shapes=[
            pltpu.VMEM((QWIDE, DEPTH), jnp.bfloat16),
            pltpu.VMEM((ROWS, CACHE, KVH * HD), jnp.bfloat16),
            pltpu.VMEM((ROWS, CACHE, KVH * HD), jnp.bfloat16),
            pltpu.VMEM((DEPTH, 512), jnp.bfloat16),
            pltpu.VMEM((2, ROWS, HD), jnp.float32),
            pltpu.VMEM(((HQ + 2 * KVH) * ROWS, HD), jnp.float32),
            pltpu.VMEM((HQ * ROWS, HD), jnp.float32),
            pltpu.SemaphoreType.DMA((4,)),
        ]
        + Projection.scratch(QWIDE, jnp.float32)
        + Projection.scratch(512, jnp.bfloat16),
        compiler_params=pltpu.CompilerParams(
            collective_id=0, has_side_effects=True, vmem_limit_bytes=60 * 1024 * 1024
        ),
        name="layer",
    )(lengths, hidden_in, norm_gain.reshape(1, -1), freqs, w_qkv.T, k_cache, v_cache, w_out)
    return blocks.transpose(1, 0, 2).reshape(ROWS, 32 * 512)


def solution(mesh):
    return jax.shard_map(
        on_device,
        mesh=mesh,
        in_specs=(
            P(("gx", "gy"), None),
            P(),
            P("gy", "gx"),
            P(("gx", "gy"), None, None),
            P(("gx", "gy"), None, None),
            P(("gx", "gy")),
            P("gy", "gx"),
        ),
        out_specs=P(("gx", "gy"), None),
        check_vma=False,
    )
```

```python
import math

import jax
import jax.numpy as jnp
from jax import lax
from jax.experimental import pallas as pl
from jax.experimental.pallas import tpu as pltpu
from jax.sharding import PartitionSpec as P

HQ = 128
KVH = 8
HD = 128
ROWS = 8
CACHE = 512
DEPTH = 4096
QWIDE = 640

eps = 1e-05
theta = 500000.0

UNITS = (
    ((0, 0), (0, 3)),
    ((0, 1), (1, 0)),
    ((3, 0), (0, 2)),
    ((1, 3), (3, 3)),
    ((1, 1), (3, 1)),
    ((2, 0), (1, 2)),
    ((3, 2), (2, 3)),
    ((2, 1), (2, 2)),
)
DIRECT = (7,)
PLACE = {ur: (w, i) for w, unit in enumerate(UNITS) for i, ur in enumerate(unit)}


def remote(src, dst, send, recv, device):
    return pltpu.make_async_remote_copy(
        src_ref=src,
        dst_ref=dst,
        send_sem=send,
        recv_sem=recv,
        device_id=device,
        device_id_type=pl.DeviceIdType.MESH,
    )


class Here:
    def __init__(self):
        gx = lax.axis_index("gx")
        self.gx = gx
        self.z = lax.axis_index("gy")
        self.y = gx // 8
        self.x = (gx // 2) % 4
        self.c = gx % 2

    def device(self, dy=0, dx=0, dc=0, dz=0):
        y = (self.y + dy) % 4
        x = (self.x + dx) % 4
        c = (self.c + dc) % 2
        return ((y * 4 + x) * 2 + c, (self.z + dz) % 4)

    def greet(self):
        barrier = pltpu.get_barrier_semaphore()
        partners = [dict(dz=1), dict(dz=3), dict(dz=2), dict(dc=1)]
        partners += [dict(dx=1), dict(dx=3), dict(dy=1), dict(dy=3)]
        for partner in partners:
            pl.semaphore_signal(
                barrier,
                inc=1,
                device_id=self.device(**partner),
                device_id_type=pl.DeviceIdType.MESH,
            )

    def greeted(self):
        pl.semaphore_wait(pltpu.get_barrier_semaphore(), 8)


class Projection:
    def __init__(self, here, refs, weight, wide, transposed):
        self.here = here
        self.weight = weight
        self.wide = wide
        self.transposed = transposed
        (
            self.mine,
            self.spread,
            self.rows,
            self.partial,
            self.relay,
            self.last,
            self.ready,
            self.owned,
            self.zsem,
            self.gsem,
            self.csem,
            self.rsem,
            self.osem,
        ) = refs
        self.sent = []

    @staticmethod
    def scratch(wide, kind):
        return [
            pltpu.VMEM((4, 8, DEPTH), jnp.bfloat16),
            pltpu.VMEM((4, 8, DEPTH), jnp.bfloat16),
            pltpu.VMEM((1024, DEPTH), jnp.bfloat16),
            pltpu.VMEM((8, 4, 32, wide), kind),
            pltpu.VMEM((8, 32, wide), kind),
            pltpu.VMEM((8, 2, 32, wide), kind),
            pltpu.VMEM((8, 4, 8, wide), jnp.bfloat16),
            pltpu.VMEM((32, 8, wide), jnp.bfloat16),
            pltpu.SemaphoreType.DMA((2, 4)),
            pltpu.SemaphoreType.DMA((2, 128)),
            pltpu.SemaphoreType.DMA((2, 32)),
            pltpu.SemaphoreType.DMA((2, 32)),
            pltpu.SemaphoreType.DMA((2, 32)),
        ]

    def push(self, *args):
        copy = remote(*args)
        copy.start()
        self.sent.append(copy)

    def exchange(self):
        z = self.here.z
        for dz in (1, 3, 2):
            to = (z + dz) % 4
            self.push(
                self.mine.at[to],
                self.spread.at[z],
                self.zsem.at[0, dz],
                self.zsem.at[1, dz],
                self.here.device(dz=dz),
            )
        self.spread[z] = self.mine[z]

    def exchanged(self):
        z = self.here.z
        for dz in (1, 3, 2):
            slot = self.spread.at[(z + 4 - dz) % 4]
            remote(
                slot, slot, self.zsem.at[0, dz], self.zsem.at[1, dz], self.here.device(dz=1)
            ).wait_recv()
        for part in range(2):
            both = jnp.concatenate([self.spread[2 * part], self.spread[2 * part + 1]], axis=0)
            self.rows[pl.ds(self.start_of(part, 0, 0, 0), 16), :] = both

    def start_of(self, part, u, r, core):
        w, i = PLACE[(u, r)]
        return w * 128 + part * 64 + (i * 2 + core) * 16

    def slot(self, part, u, r, core, half=None):
        columns = pl.ds(0, DEPTH) if half is None else pl.ds(half * (DEPTH // 2), DEPTH // 2)
        return self.rows.at[pl.ds(self.start_of(part, u, r, core), 16), columns]

    def gather_sem(self, side, part, u, r, half):
        return self.gsem.at[side, ((part * 4 + u) * 4 + r) * 2 + (half or 0)]

    def along(self, part, first, step):
        if first == (part == 0):
            return self.here.device(dx=step)
        return self.here.device(dy=step)

    def hop(self, part, u, r, first, step, half=None):
        nu, nr = (u, (r - step) % 4) if first else ((u - step) % 4, r)
        self.push(
            self.slot(part, u, r, 0, half),
            self.slot(part, nu, nr, 0, half),
            self.gather_sem(0, part, nu, nr, half),
            self.gather_sem(1, part, nu, nr, half),
            self.along(part, first, step),
        )

    def to_sibling(self, part, u, r):
        k = (part * 4 + u) * 4 + r
        self.push(
            self.slot(part, u, r, 0),
            self.slot(part, u, r, 1),
            self.csem.at[0, k],
            self.csem.at[1, k],
            self.here.device(dc=1),
        )

    def arrived(self, part, u, r):
        halves = (0, 1) if (u == 2 or (u == 0 and r == 2)) else (None,)
        for half in halves:
            slot = self.slot(part, u, r, 0, half)
            remote(
                slot,
                slot,
                self.gather_sem(0, part, u, r, half),
                self.gather_sem(1, part, u, r, half),
                self.here.device(dc=1),
            ).wait_recv()

    def sibling_arrived(self, part, u, r):
        k = (part * 4 + u) * 4 + r
        slot = self.slot(part, u, r, 1)
        remote(
            slot, slot, self.csem.at[0, k], self.csem.at[1, k], self.here.device(dc=1)
        ).wait_recv()

    def start(self):
        for first in (True, False):
            for part in range(2):
                self.hop(part, 0, 0, first, 1)
                self.hop(part, 0, 0, first, -1)
        for part in range(2):
            self.to_sibling(part, 0, 0)

    def second(self, r):
        for part in range(2):
            self.hop(part, 0, r, False, 1)
            self.hop(part, 0, r, False, -1)

    def take(self, u, r):
        for part in range(2):
            self.arrived(part, u, r)
            if u in (1, 3):
                self.hop(part, u, r, False, 1 if u == 3 else -1, 0 if u == 3 else 1)
            elif u == 0 and r in (1, 3):
                self.hop(part, u, r, True, 1 if r == 3 else -1, 0 if r == 3 else 1)
            self.to_sibling(part, u, r)

    def dots(self, w):
        for u, r in UNITS[w]:
            for part in range(2):
                self.sibling_arrived(part, u, r)

        def tile(start, width):
            lhs = self.rows[pl.ds(w * 128, 128), :]
            if self.transposed:
                out = lax.dot_general(
                    lhs,
                    self.weight[pl.ds(start, width), :],
                    (((1,), (1,)), ((), ())),
                    preferred_element_type=jnp.float32,
                )
            else:
                out = jnp.dot(
                    lhs,
                    self.weight[:, pl.ds(start, width)],
                    preferred_element_type=jnp.float32,
                )
            out = out.reshape(2, 4, 2, 8, width)
            for d in range(4):
                self.partial[w, d, :, pl.ds(start, width)] = (
                    out[d // 2, :, d % 2].reshape(32, width).astype(self.partial.dtype)
                )

        @pl.loop(0, self.wide // 256)
        def _(n):
            tile(pl.multiple_of(n * 256, 256), 256)

        if self.wide % 256:
            tile(self.wide // 256 * 256, self.wide % 256)

    def ring_copy(self, src, dst, k, dz):
        self.push(src, dst, self.rsem.at[0, k], self.rsem.at[1, k], self.here.device(dz=dz))

    def ring_wait(self, dst, k):
        remote(
            dst, dst, self.rsem.at[0, k], self.rsem.at[1, k], self.here.device(dz=1)
        ).wait_recv()

    def relay_out(self, w):
        z = self.here.z
        far = (z + 2) % 4
        if w in DIRECT:
            for side, dz in ((0, 1), (1, -1)):
                to = (z + dz) % 4
                self.ring_copy(self.partial.at[w, to], self.last.at[w, side], w * 4 + 2 + side, dz)
            self.ring_copy(self.partial.at[w, far], self.relay.at[w], w * 4, 2)
            return
        for side, dz in ((0, 1), (1, -1)):
            self.ring_copy(
                self.partial.at[w, far, pl.ds(16 * side, 16)],
                self.relay.at[w, pl.ds(16 * side, 16)],
                w * 4 + side,
                dz,
            )

    def neighbours_out(self, w):
        if w in DIRECT:
            return
        for side, dz in ((0, 1), (1, -1)):
            to = (self.here.z + dz) % 4
            half = pl.ds(16 * side, 16)
            self.ring_wait(self.relay.at[w, half], w * 4 + side)
            total = self.partial[w, to, half, :].astype(jnp.float32) + self.relay[
                w, half, :
            ].astype(jnp.float32)
            self.partial[w, to, half, :] = total.astype(self.partial.dtype)
            self.ring_copy(self.partial.at[w, to], self.last.at[w, side], w * 4 + 2 + side, dz)

    def owners_out(self, w):
        here = self.here
        total = self.partial[w, here.z].astype(jnp.float32)
        for side in range(2):
            self.ring_wait(self.last.at[w, side], w * 4 + 2 + side)
            total = total + self.last[w, side].astype(jnp.float32)
        if w in DIRECT:
            self.ring_wait(self.relay.at[w], w * 4)
            total = total + self.relay[w].astype(jnp.float32)
        self.ready[w] = total.reshape(4, 8, self.wide).astype(jnp.bfloat16)
        for i, (u, r) in enumerate(UNITS[w]):
            for core in range(2):
                j = i * 2 + core
                if w == 0 and j == 0:
                    self.owned[here.gx] = self.ready[0, 0]
                    continue
                self.push(
                    self.ready.at[w, j],
                    self.owned.at[here.gx],
                    self.osem.at[0, w * 4 + j],
                    self.osem.at[1, w * 4 + j],
                    self.owner(u, r, core),
                )

    def owner(self, u, r, core):
        first = self.here.z < 2
        dy = jnp.where(first, u, r)
        dx = jnp.where(first, r, u)
        return self.here.device(dy, dx, core)

    def owners_in(self):
        for w in range(8):
            for i, (u, r) in enumerate(UNITS[w]):
                for core in range(2):
                    j = i * 2 + core
                    if w == 0 and j == 0:
                        continue
                    source, _ = self.owner(4 - u, 4 - r, core)
                    slot = self.owned.at[source]
                    remote(
                        slot,
                        slot,
                        self.osem.at[0, w * 4 + j],
                        self.osem.at[1, w * 4 + j],
                        self.here.device(dc=1),
                    ).wait_recv()

    def run(self, weight_in):
        self.exchanged()
        self.start()
        self.take(0, 3)
        self.take(0, 1)
        self.second(3)
        self.second(1)
        weight_in()
        self.unit(0)
        self.take(3, 0)
        self.take(1, 0)
        self.unit(1)
        self.take(0, 2)
        self.second(2)
        self.neighbours_out(0)
        self.unit(2)
        self.take(3, 3)
        self.take(1, 3)
        self.neighbours_out(1)
        self.unit(3)
        self.take(3, 1)
        self.take(1, 1)
        self.neighbours_out(2)
        self.owners_out(0)
        self.unit(4)
        self.take(2, 0)
        self.take(3, 2)
        self.take(1, 2)
        self.neighbours_out(3)
        self.owners_out(1)
        self.unit(5)
        self.take(2, 3)
        self.neighbours_out(4)
        self.owners_out(2)
        self.unit(6)
        self.take(2, 1)
        self.take(2, 2)
        self.neighbours_out(5)
        self.owners_out(3)
        self.unit(7)
        self.neighbours_out(6)
        self.owners_out(4)
        self.owners_out(5)
        self.owners_out(6)
        self.owners_out(7)
        self.owners_in()

    def unit(self, w):
        self.dots(w)
        self.relay_out(w)

    def finish(self):
        for copy in self.sent:
            copy.wait_send()


def normalized(step, hidden, gain):
    widened = hidden[...].astype(jnp.float32)
    scale = lax.rsqrt(jnp.mean(widened * widened, axis=-1, keepdims=True) + eps)
    for z in range(4):
        columns = pl.ds(z * DEPTH, DEPTH)
        step.mine[z] = (hidden[:, columns].astype(jnp.float32) * scale * gain[:, columns]).astype(
            jnp.bfloat16
        )


def turn(lengths, freqs, turns):
    row = lax.broadcasted_iota(jnp.int32, (ROWS, HD), 0)
    lane = lax.broadcasted_iota(jnp.int32, (ROWS, HD), 1)
    position = jnp.zeros((ROWS, HD), jnp.float32)
    for r in range(ROWS):
        position = jnp.where(row == r, lengths[r].astype(jnp.float32), position)
    angle = position * freqs[...]
    turns[0] = jnp.cos(angle)
    turns[1] = jnp.where(lane < HD // 2, -jnp.sin(angle), jnp.sin(angle))


def heads(owned, turns, qkv):
    lane = lax.broadcasted_iota(jnp.int32, (ROWS, HD), 1)
    for pair in range(16):
        even = owned[2 * pair].astype(jnp.float32)
        odd = owned[2 * pair + 1].astype(jnp.float32)
        for t in range(9):
            if t < 4:
                head = even[:, t * HD : (t + 1) * HD]
            elif t > 4:
                head = odd[:, (t - 4) * HD : (t - 3) * HD]
            else:
                head = jnp.where(lane < HD // 2, even[:, 4 * HD :], odd[:, :HD])
            h = pair * 9 + t
            if h < HQ + KVH:
                head = head * turns[0] + pltpu.roll(head, HD // 2, 1) * turns[1]
                head = head.astype(jnp.bfloat16).astype(jnp.float32)
            qkv[pl.ds(h * ROWS, ROWS), :] = head


def attend(lengths, keys, values, qkv, scored, weighed, mixed, out):
    share = HQ // KVH
    scale = 1.0 / math.sqrt(HD)

    @pl.loop(0, ROWS)
    def _(r):
        for g in range(KVH):
            query = qkv[pl.ds(g * share * ROWS + r, share, stride=ROWS), :]
            scored[r, pl.ds(g * share, share), :] = (
                lax.dot_general(
                    query.astype(jnp.bfloat16),
                    keys[r, :, pl.ds(g * HD, HD)],
                    (((1,), (1,)), ((), ())),
                    preferred_element_type=jnp.float32,
                )
                * scale
            )

    @pl.loop(0, ROWS)
    def _(r):
        valid = lax.broadcasted_iota(jnp.int32, (HQ, CACHE), 1) < lengths[r]
        query = qkv[pl.ds(r, HQ, stride=ROWS), :]
        key_new = qkv[pl.ds(HQ * ROWS + r, KVH, stride=ROWS), :]
        value_new = qkv[pl.ds((HQ + KVH) * ROWS + r, KVH, stride=ROWS), :]
        both = query.reshape(KVH, share, HD) * key_new.reshape(KVH, 1, HD)
        fresh = jnp.sum(both.reshape(HQ, HD), axis=1, keepdims=True) * scale
        scores = jnp.where(valid, scored[r], -jnp.inf)
        top = jnp.maximum(jnp.max(scores, axis=1, keepdims=True), fresh)
        probs = jnp.exp(scores - top)
        pnew = jnp.exp(fresh - top)
        total = jnp.sum(probs, axis=1, keepdims=True) + pnew
        weighed[r] = (probs / total).astype(jnp.bfloat16)
        wnew = (pnew / total).astype(jnp.bfloat16).astype(jnp.float32)
        added = wnew.reshape(KVH, share, 1) * value_new.reshape(KVH, 1, HD)
        mixed[pl.ds(r, HQ, stride=ROWS), :] = added.reshape(HQ, HD)

    @pl.loop(0, ROWS)
    def _(r):
        for g in range(KVH):
            span = pl.ds(g * share * ROWS + r, share, stride=ROWS)
            mixed[span, :] = mixed[span, :] + jnp.dot(
                weighed[r, pl.ds(g * share, share), :],
                values[r, :, pl.ds(g * HD, HD)],
                preferred_element_type=jnp.float32,
            )

    for h in range(HQ):
        out[h // 32, :, pl.ds(h % 32 * HD, HD)] = mixed[pl.ds(h * ROWS, ROWS), :].astype(
            jnp.bfloat16
        )


def layer(
    lengths,
    hidden,
    gain,
    freqs,
    w_qkv,
    k_cache,
    v_cache,
    w_out,
    out,
    weight_in,
    keys,
    values,
    weight_out,
    turns,
    qkv,
    scored,
    weighed,
    mixed,
    loads,
    *refs,
):
    here = Here()
    here.greet()
    count = len(refs) // 2
    first = Projection(here, refs[:count], weight_in, QWIDE, True)
    second = Projection(here, refs[count:], weight_out, 512, False)
    fetch = [
        pltpu.make_async_copy(
            w_qkv, weight_in.at[pl.ds(pl.multiple_of(here.c * 64, 64), 576), :], loads.at[0]
        ),
        pltpu.make_async_copy(k_cache, keys, loads.at[1]),
        pltpu.make_async_copy(v_cache, values, loads.at[2]),
        pltpu.make_async_copy(w_out, weight_out, loads.at[3]),
    ]
    for copy in fetch:
        copy.start()
    weight_in[pl.ds(pl.multiple_of((1 - here.c) * 576, 64), 64), :] = jnp.zeros(
        (64, DEPTH), jnp.bfloat16
    )
    normalized(first, hidden, gain)
    here.greeted()
    first.exchange()
    turn(lengths, freqs, turns)
    first.run(fetch[0].wait)
    heads(first.owned, turns, qkv)
    fetch[1].wait()
    fetch[2].wait()
    attend(lengths, keys, values, qkv, scored, weighed, mixed, second.mine)
    second.exchange()
    second.run(fetch[3].wait)
    out[...] = second.owned[...]
    first.finish()
    second.finish()


def on_device(hidden_in, norm_gain, w_qkv, k_cache, v_cache, lengths, w_out):
    half = jnp.arange(HD // 2, dtype=jnp.float32)
    freqs = theta ** (-2.0 * half / HD)
    freqs = jnp.concatenate([freqs, freqs]).reshape(1, HD)
    vmem = pl.BlockSpec(memory_space=pltpu.VMEM)
    hbm = pl.BlockSpec(memory_space=pl.ANY)
    blocks = pl.pallas_call(
        layer,
        out_shape=jax.ShapeDtypeStruct((32, ROWS, 512), jnp.bfloat16),
        in_specs=[pl.BlockSpec(memory_space=pltpu.SMEM), vmem, vmem, vmem, hbm, hbm, hbm, hbm],
        out_specs=vmem,
        scratch_shapes=[
            pltpu.VMEM((QWIDE, DEPTH), jnp.bfloat16),
            pltpu.VMEM((ROWS, CACHE, KVH * HD), jnp.bfloat16),
            pltpu.VMEM((ROWS, CACHE, KVH * HD), jnp.bfloat16),
            pltpu.VMEM((DEPTH, 512), jnp.bfloat16),
            pltpu.VMEM((2, ROWS, HD), jnp.float32),
            pltpu.VMEM(((HQ + 2 * KVH) * ROWS, HD), jnp.float32),
            pltpu.VMEM((ROWS, HQ, CACHE), jnp.float32),
            pltpu.VMEM((ROWS, HQ, CACHE), jnp.bfloat16),
            pltpu.VMEM((HQ * ROWS, HD), jnp.float32),
            pltpu.SemaphoreType.DMA((4,)),
        ]
        + Projection.scratch(QWIDE, jnp.float32)
        + Projection.scratch(512, jnp.bfloat16),
        compiler_params=pltpu.CompilerParams(
            collective_id=0, has_side_effects=True, vmem_limit_bytes=60 * 1024 * 1024
        ),
        name="layer",
    )(lengths, hidden_in, norm_gain.reshape(1, -1), freqs, w_qkv.T, k_cache, v_cache, w_out)
    return blocks.transpose(1, 0, 2).reshape(ROWS, 32 * 512)


def solution(mesh):
    return jax.shard_map(
        on_device,
        mesh=mesh,
        in_specs=(
            P(("gx", "gy"), None),
            P(),
            P("gy", "gx"),
            P(("gx", "gy"), None, None),
            P(("gx", "gy"), None, None),
            P(("gx", "gy")),
            P("gy", "gx"),
        ),
        out_specs=P(("gx", "gy"), None),
        check_vma=False,
    )
```

```python
import math

import jax
import jax.numpy as jnp
import numpy as np
from jax import lax
from jax.experimental import pallas as pl
from jax.experimental.pallas import tpu as pltpu
from jax.sharding import PartitionSpec as P

HQ = 128
KVH = 8
HD = 128
ROWS = 8
CACHE = 512
DEPTH = 4096
QWIDE = 640

eps = 1e-05
theta = 500000.0

UNITS = (
    ((0, 0), (0, 3)),
    ((0, 1), (1, 0)),
    ((3, 0), (0, 2)),
    ((1, 3), (3, 3)),
    ((1, 1), (3, 1)),
    ((2, 0), (1, 2)),
    ((3, 2), (2, 3)),
    ((2, 1), (2, 2)),
)
DIRECT = (7,)
PLACE = {ur: (w, i) for w, unit in enumerate(UNITS) for i, ur in enumerate(unit)}


def remote(src, dst, send, recv, device):
    return pltpu.make_async_remote_copy(
        src_ref=src,
        dst_ref=dst,
        send_sem=send,
        recv_sem=recv,
        device_id=device,
        device_id_type=pl.DeviceIdType.MESH,
    )


class Here:
    def __init__(self):
        gx = lax.axis_index("gx")
        self.gx = gx
        self.z = lax.axis_index("gy")
        self.y = gx // 8
        self.x = (gx // 2) % 4
        self.c = gx % 2

    def device(self, dy=0, dx=0, dc=0, dz=0):
        y = (self.y + dy) % 4
        x = (self.x + dx) % 4
        c = (self.c + dc) % 2
        return ((y * 4 + x) * 2 + c, (self.z + dz) % 4)

    def greet(self):
        barrier = pltpu.get_barrier_semaphore()
        partners = [dict(dz=1), dict(dz=3), dict(dz=2), dict(dc=1)]
        partners += [dict(dx=1), dict(dx=3), dict(dy=1), dict(dy=3)]
        for partner in partners:
            pl.semaphore_signal(
                barrier,
                inc=1,
                device_id=self.device(**partner),
                device_id_type=pl.DeviceIdType.MESH,
            )

    def greeted(self):
        pl.semaphore_wait(pltpu.get_barrier_semaphore(), 8)


class Projection:
    def __init__(self, here, refs, rows, sems, weight, shared=None):
        self.here = here
        self.weight = weight
        self.shared = shared
        self.rows = rows
        self.mine, self.spread, self.partial, self.relay, self.last, self.ready, self.owned = refs
        self.tall = self.partial.shape[2]
        self.wide = self.owned.shape[2]
        self.got_z, self.got_near, self.got_far = (sems.at[k] for k in range(3))
        self.got_shard = lambda u, r: sems.at[3 + u * 4 + r]
        self.got_sibling = lambda w: sems.at[19 + w]
        self.got_relay = lambda w: sems.at[27 + w]
        self.got_last = lambda w: sems.at[35 + w]
        self.put_z, self.put_shard, self.put_sibling, self.put_sum, self.put_near, self.put_far = (
            sems.at[43 + k] for k in range(6)
        )

    SEMAPHORES = 49

    @staticmethod
    def scratch(wide, kind):
        tall = 128 if wide == 512 else 144
        return [
            pltpu.VMEM((4, 8, DEPTH), jnp.bfloat16),
            pltpu.VMEM((4, 8, DEPTH), jnp.bfloat16),
            pltpu.VMEM((8, 4, tall, HD), kind),
            pltpu.VMEM((8, tall, HD), kind),
            pltpu.VMEM((8, 2, tall, HD), kind),
            pltpu.VMEM((8, 4, 8, wide), jnp.bfloat16),
            pltpu.VMEM((32, 8, wide), jnp.bfloat16),
        ]

    def wait(self, ref, sem):
        remote(ref, ref, self.put_z, sem, self.here.device(dc=1)).wait_recv()

    def exchange(self):
        z = self.here.z
        for dz in (2, 1, 3):
            to = (z + dz) % 4
            remote(
                self.mine.at[to],
                self.spread.at[z],
                self.put_z,
                self.got_z,
                self.here.device(dz=dz),
            ).start()
        self.spread[z] = self.mine[z]

    def exchanged(self):
        self.wait(self.spread.at[pl.ds(0, 3)], self.got_z)
        for part in range(2):
            both = jnp.concatenate([self.spread[2 * part], self.spread[2 * part + 1]], axis=0)
            self.rows[pl.ds(self.start_of(0, 0, 0) + 16 * part, 16), :] = both

    @staticmethod
    def start_of(u, r, core):
        w, i = PLACE[(u, r)]
        return w * 128 + (i * 2 + core) * 32

    def slot(self, part, u, r, half=None):
        columns = pl.ds(0, DEPTH) if half is None else pl.ds(half * (DEPTH // 2), DEPTH // 2)
        return self.rows.at[pl.ds(self.start_of(u, r, 0) + part * 16, 16), columns]

    def hop(self, u, r, first, step, half=None):
        nu, nr = (u, (r - step) % 4) if first else ((u - step) % 4, r)
        for part in range(2):
            along = dict(dx=step) if first == (part == 0) else dict(dy=step)
            remote(
                self.slot(part, u, r, half),
                self.slot(part, nu, nr, half),
                self.put_shard,
                self.got_shard(nu, nr),
                self.here.device(**along),
            ).start()

    def to_sibling(self, u, r):
        remote(
            self.rows.at[pl.ds(self.start_of(u, r, 0), 32)],
            self.rows.at[pl.ds(self.start_of(u, r, 1), 32)],
            self.put_sibling,
            self.got_sibling(PLACE[(u, r)][0]),
            self.here.device(dc=1),
        ).start()

    def start(self):
        for first in (True, False):
            self.hop(0, 0, first, 1)
            self.hop(0, 0, first, -1)
        self.to_sibling(0, 0)

    def second(self, r):
        self.hop(0, r, False, 1)
        self.hop(0, r, False, -1)

    def take(self, u, r):
        self.wait(self.rows.at[pl.ds(self.start_of(u, r, 0), 32)], self.got_shard(u, r))
        if u in (1, 3):
            self.hop(u, r, False, 1 if u == 3 else -1, 0 if u == 3 else 1)
        elif u == 0 and r in (1, 3):
            self.hop(u, r, True, 1 if r == 3 else -1, 0 if r == 3 else 1)
        self.to_sibling(u, r)

    def dots(self, w):
        self.wait(self.rows.at[pl.ds(w * 128, 64)], self.got_sibling(w))

        @pl.loop(0, 2)
        def _(n):
            out = jnp.dot(
                self.rows[pl.ds(w * 128, 128), :],
                self.weight[:, pl.ds(pl.multiple_of(n * 256, 256), 256)],
                preferred_element_type=jnp.float32,
            ).reshape(4, 4, 8, 256)
            for d in range(4):
                for m in range(2):
                    block = out[:, d, :, m * HD : (m + 1) * HD].reshape(32, HD)
                    at = pl.ds(pl.multiple_of(n * 64 + m * 32, 32), 32)
                    self.partial[w, d, at, :] = block.astype(self.partial.dtype)

        if self.shared is not None:
            own = jnp.concatenate(
                [self.rows[pl.ds(w * 128 + i * 64, 32), :] for i in range(2)], axis=0
            )
            out = lax.dot_general(
                own, self.shared[...], (((1,), (1,)), ((), ())), preferred_element_type=jnp.float32
            ).reshape(2, 4, 8, HD)
            for d in range(4):
                self.partial[w, d, pl.ds(128, 16), :] = out[:, d].reshape(16, HD)

    def sum_copy(self, src, dst, sem, dz):
        remote(src, dst, self.put_sum, sem, self.here.device(dz=dz)).start()

    def relay_out(self, w):
        z = self.here.z
        far = (z + 2) % 4
        half = self.tall // 2
        if w in DIRECT:
            self.sum_copy(self.partial.at[w, far], self.relay.at[w], self.got_relay(w), 2)
            for side, dz in ((0, 1), (1, -1)):
                to = (z + dz) % 4
                self.sum_copy(
                    self.partial.at[w, to], self.last.at[w, side], self.got_last(w), dz
                )
            return
        for side, dz in ((0, 1), (1, -1)):
            at = pl.ds(half * side, half)
            self.sum_copy(
                self.partial.at[w, far, at], self.relay.at[w, at], self.got_relay(w), dz
            )

    def neighbours_out(self, w):
        if w in DIRECT:
            return
        self.wait(self.relay.at[w], self.got_relay(w))
        half = self.tall // 2
        for side, dz in ((0, 1), (1, -1)):
            to = (self.here.z + dz) % 4
            at = pl.ds(half * side, half)
            total = self.partial[w, to, at, :].astype(jnp.float32) + self.relay[w, at, :].astype(
                jnp.float32
            )
            self.partial[w, to, at, :] = total.astype(self.partial.dtype)
            self.sum_copy(self.partial.at[w, to], self.last.at[w, side], self.got_last(w), dz)

    def owners_out(self, w):
        here = self.here
        self.wait(self.last.at[w], self.got_last(w))
        total = self.partial[w, here.z].astype(jnp.float32)
        for side in range(2):
            total = total + self.last[w, side].astype(jnp.float32)
        if w in DIRECT:
            self.wait(self.relay.at[w], self.got_relay(w))
            total = total + self.relay[w].astype(jnp.float32)
        total = total.astype(jnp.bfloat16).astype(jnp.float32)
        for n in range(4):
            block = total[n * 32 : (n + 1) * 32].reshape(4, 8, HD)
            self.ready[w, :, :, pl.ds(n * HD, HD)] = block.astype(jnp.bfloat16)
        if self.shared is not None:
            for i in range(2):
                block = total[128 + i * 8 : 136 + i * 8]
                self.ready[w, 2 * i, :, pl.ds(512, HD)] = block.astype(jnp.bfloat16)
        for i, (u, r) in enumerate(UNITS[w]):
            for core in range(2):
                j = i * 2 + core
                if w == 0 and j == 0:
                    self.owned[here.gx] = self.ready[0, 0]
                    continue
                wide = pl.ds(0, 512 if core else self.wide)
                remote(
                    self.ready.at[w, j, :, wide],
                    self.owned.at[here.gx, :, wide],
                    self.put_far if core else self.put_near,
                    self.got_far if core else self.got_near,
                    self.owner(u, r, core),
                ).start()

    def owner(self, u, r, core):
        first = self.here.z < 2
        dy = jnp.where(first, u, r)
        dx = jnp.where(first, r, u)
        return self.here.device(dy, dx, core)

    def near(self):
        return self.owned.at[pl.ds(0, 15)]

    def far(self):
        return self.owned.at[pl.ds(0, 16), :, pl.ds(0, 512)]

    def owners_in(self):
        self.wait(self.near(), self.got_near)
        self.wait(self.far(), self.got_far)

    def unit(self, w):
        self.dots(w)
        self.relay_out(w)

    def run(self, weight_in):
        self.exchanged()
        self.start()
        self.take(0, 3)
        self.take(0, 1)
        self.second(3)
        self.second(1)
        weight_in()
        self.unit(0)
        self.take(3, 0)
        self.take(1, 0)
        self.unit(1)
        self.take(0, 2)
        self.second(2)
        self.neighbours_out(0)
        self.unit(2)
        self.take(3, 3)
        self.take(1, 3)
        self.neighbours_out(1)
        self.unit(3)
        self.neighbours_out(2)
        self.take(3, 1)
        self.take(1, 1)
        self.owners_out(0)
        self.unit(4)
        self.neighbours_out(3)
        self.take(2, 0)
        self.take(3, 2)
        self.take(1, 2)
        self.owners_out(1)
        self.unit(5)
        self.take(2, 3)
        self.neighbours_out(4)
        self.owners_out(2)
        self.unit(6)
        self.neighbours_out(5)
        self.take(2, 1)
        self.take(2, 2)
        self.unit(7)
        self.owners_out(3)
        self.neighbours_out(6)
        self.owners_out(4)
        self.owners_out(5)
        self.owners_out(6)
        self.owners_out(7)
        self.owners_in()

    def finish(self):
        for ref, sem in (
            (self.mine.at[pl.ds(0, 3)], self.put_z),
            (self.rows.at[pl.ds(0, 480)], self.put_shard),
            (self.rows.at[pl.ds(0, 512)], self.put_sibling),
            (self.partial.at[pl.ds(0, 6)], self.put_sum),
            (self.near(), self.put_near),
            (self.far(), self.put_far),
        ):
            remote(ref, ref, sem, self.got_z, self.here.device(dc=1)).wait_send()


def normalized(step, hidden, gain):
    widened = hidden[...].astype(jnp.float32)
    scale = lax.rsqrt(jnp.mean(widened * widened, axis=-1, keepdims=True) + eps)
    for z in range(4):
        columns = pl.ds(z * DEPTH, DEPTH)
        step.mine[z] = (hidden[:, columns].astype(jnp.float32) * scale * gain[:, columns]).astype(
            jnp.bfloat16
        )


def turn(lengths, freqs, turns):
    row = lax.broadcasted_iota(jnp.int32, (ROWS, HD), 0)
    lane = lax.broadcasted_iota(jnp.int32, (ROWS, HD), 1)
    position = jnp.zeros((ROWS, HD), jnp.float32)
    for r in range(ROWS):
        position = jnp.where(row == r, lengths[r].astype(jnp.float32), position)
    angle = position * freqs[...]
    turns[0] = jnp.cos(angle)
    turns[1] = jnp.where(lane < HD // 2, -jnp.sin(angle), jnp.sin(angle))


def heads(core, owned, turns, qkv):
    for pair in range(16):
        even = owned[2 * pair, :, pl.ds(0, 512)].astype(jnp.float32)
        odd = owned[2 * pair + 1, :, pl.ds(0, 512)].astype(jnp.float32)
        between = owned[2 * pair + core, :, pl.ds(512, HD)].astype(jnp.float32)
        for t in range(9):
            if t < 4:
                head = even[:, t * HD : (t + 1) * HD]
            elif t > 4:
                head = odd[:, (t - 5) * HD : (t - 4) * HD]
            else:
                head = between
            h = pair * 9 + t
            if h < HQ + KVH:
                head = head * turns[0] + pltpu.roll(head, HD // 2, 1) * turns[1]
                head = head.astype(jnp.bfloat16).astype(jnp.float32)
            qkv[pl.ds(h * ROWS, ROWS), :] = head


def attend(lengths, keys, values, qkv, scored, weighed, mixed, out):
    share = HQ // KVH
    scale = 1.0 / math.sqrt(HD)

    @pl.loop(0, ROWS)
    def _(r):
        for g in range(KVH):
            query = qkv[pl.ds(g * share * ROWS + r, share, stride=ROWS), :]
            scored[r, pl.ds(g * share, share), :] = (
                lax.dot_general(
                    query.astype(jnp.bfloat16),
                    keys[r, :, pl.ds(g * HD, HD)],
                    (((1,), (1,)), ((), ())),
                    preferred_element_type=jnp.float32,
                )
                * scale
            )

    @pl.loop(0, ROWS)
    def _(r):
        valid = lax.broadcasted_iota(jnp.int32, (HQ, CACHE), 1) < lengths[r]
        query = qkv[pl.ds(r, HQ, stride=ROWS), :]
        key_new = qkv[pl.ds(HQ * ROWS + r, KVH, stride=ROWS), :]
        value_new = qkv[pl.ds((HQ + KVH) * ROWS + r, KVH, stride=ROWS), :]
        both = query.reshape(KVH, share, HD) * key_new.reshape(KVH, 1, HD)
        fresh = jnp.sum(both.reshape(HQ, HD), axis=1, keepdims=True) * scale
        scores = jnp.where(valid, scored[r], -jnp.inf)
        top = jnp.maximum(jnp.max(scores, axis=1, keepdims=True), fresh)
        probs = jnp.exp(scores - top)
        pnew = jnp.exp(fresh - top)
        total = jnp.sum(probs, axis=1, keepdims=True) + pnew
        weighed[r] = (probs / total).astype(jnp.bfloat16)
        wnew = (pnew / total).astype(jnp.bfloat16).astype(jnp.float32)
        added = wnew.reshape(KVH, share, 1) * value_new.reshape(KVH, 1, HD)
        mixed[pl.ds(r, HQ, stride=ROWS), :] = added.reshape(HQ, HD)

    @pl.loop(0, ROWS)
    def _(r):
        for g in range(KVH):
            span = pl.ds(g * share * ROWS + r, share, stride=ROWS)
            mixed[span, :] = mixed[span, :] + jnp.dot(
                weighed[r, pl.ds(g * share, share), :],
                values[r, :, pl.ds(g * HD, HD)],
                preferred_element_type=jnp.float32,
            )

    for h in range(HQ):
        out[h // 32, :, pl.ds(h % 32 * HD, HD)] = mixed[pl.ds(h * ROWS, ROWS), :].astype(
            jnp.bfloat16
        )


def transposed(raw, weight):
    @pl.loop(0, DEPTH // 512)
    def _(k):
        for n in range(4):
            at = pl.ds(pl.multiple_of(k * 512, 512), 512)
            weight[at, pl.ds(n * HD, HD)] = raw[pl.ds(n * HD, HD), at].T


def layer(
    lengths,
    hidden,
    gain,
    freqs,
    w_qkv,
    k_cache,
    v_cache,
    w_out,
    out,
    later_rows,
    shared,
    weight_in,
    keys,
    values,
    weight_out,
    turns,
    qkv,
    scored,
    weighed,
    mixed,
    rows,
    loads,
    sems,
    *refs,
):
    here = Here()
    here.greet()
    count = len(refs) // 2
    first = Projection(here, refs[:count], rows, sems, weight_in, shared)
    second = Projection(here, refs[count:], later_rows, sems, weight_out)
    raw = later_rows.at[pl.ds(0, 512)]
    c = here.c
    half = w_qkv.at[pl.ds(pl.multiple_of((1 - c) * 512, 64), 64)]
    place = shared.at[pl.ds(pl.multiple_of(c * 64, 64), 64)]
    fetch = [
        pltpu.make_async_copy(
            w_qkv.at[pl.ds(pl.multiple_of(c * 64, 64), 512)], raw, loads.at[0]
        ),
        pltpu.make_async_copy(half, place, loads.at[1]),
        pltpu.make_async_copy(k_cache, keys, loads.at[2]),
        pltpu.make_async_copy(v_cache, values, loads.at[3]),
        pltpu.make_async_copy(w_out, weight_out, loads.at[4]),
    ]
    for copy in fetch:
        copy.start()
    normalized(first, hidden, gain)
    here.greeted()
    first.exchange()
    swap = remote(half, place, loads.at[5], loads.at[6], here.device(dc=1))
    swap.start()
    turn(lengths, freqs, turns)
    fetch[0].wait()
    transposed(raw, weight_in)
    fetch[1].wait()
    first.run(swap.wait)
    heads(c, first.owned, turns, qkv)
    fetch[2].wait()
    fetch[3].wait()
    attend(lengths, keys, values, qkv, scored, weighed, mixed, second.mine)
    first.finish()
    second.exchange()
    second.run(fetch[4].wait)
    out[...] = second.owned[...]
    second.finish()


def on_device(hidden_in, norm_gain, w_qkv, k_cache, v_cache, lengths, w_out):
    freqs = theta ** (-2.0 * (np.arange(HD) % (HD // 2)) / HD)
    freqs = jnp.asarray(freqs.astype(np.float32).reshape(1, HD))
    vmem = pl.BlockSpec(memory_space=pltpu.VMEM)
    hbm = pl.BlockSpec(memory_space=pl.ANY)
    blocks = pl.pallas_call(
        layer,
        out_shape=jax.ShapeDtypeStruct((32, ROWS, 512), jnp.bfloat16),
        in_specs=[pl.BlockSpec(memory_space=pltpu.SMEM), vmem, vmem, vmem, hbm, hbm, hbm, hbm],
        out_specs=vmem,
        scratch_shapes=[
            pltpu.VMEM((1024, DEPTH), jnp.bfloat16),
            pltpu.VMEM((HD, DEPTH), jnp.bfloat16),
            pltpu.VMEM((DEPTH, 512), jnp.bfloat16),
            pltpu.VMEM((ROWS, CACHE, KVH * HD), jnp.bfloat16),
            pltpu.VMEM((ROWS, CACHE, KVH * HD), jnp.bfloat16),
            pltpu.VMEM((DEPTH, 512), jnp.bfloat16),
            pltpu.VMEM((2, ROWS, HD), jnp.float32),
            pltpu.VMEM(((HQ + 2 * KVH) * ROWS, HD), jnp.float32),
            pltpu.VMEM((ROWS, HQ, CACHE), jnp.float32),
            pltpu.VMEM((ROWS, HQ, CACHE), jnp.bfloat16),
            pltpu.VMEM((HQ * ROWS, HD), jnp.float32),
            pltpu.VMEM((1024, DEPTH), jnp.bfloat16),
            pltpu.SemaphoreType.DMA((7,)),
            pltpu.SemaphoreType.DMA((Projection.SEMAPHORES,)),
        ]
        + Projection.scratch(QWIDE, jnp.float32)
        + Projection.scratch(512, jnp.bfloat16),
        compiler_params=pltpu.CompilerParams(
            collective_id=0, has_side_effects=True, vmem_limit_bytes=60 * 1024 * 1024
        ),
        name="layer",
    )(lengths, hidden_in, norm_gain.reshape(1, -1), freqs, w_qkv.T, k_cache, v_cache, w_out)
    return blocks.transpose(1, 0, 2).reshape(ROWS, 32 * 512)


def solution(mesh):
    return jax.shard_map(
        on_device,
        mesh=mesh,
        in_specs=(
            P(("gx", "gy"), None),
            P(),
            P("gy", "gx"),
            P(("gx", "gy"), None, None),
            P(("gx", "gy"), None, None),
            P(("gx", "gy")),
            P("gy", "gx"),
        ),
        out_specs=P(("gx", "gy"), None),
        check_vma=False,
    )
```

```python
import math

import jax
import jax.numpy as jnp
import numpy as np
from jax import lax
from jax.experimental import pallas as pl
from jax.experimental.pallas import tpu as pltpu
from jax.sharding import PartitionSpec as P

HQ = 128
KVH = 8
HD = 128
ROWS = 8
CACHE = 512
DEPTH = 4096
QWIDE = 640

eps = 1e-05
theta = 500000.0

UNITS = (
    ((0, 0), (0, 3)),
    ((0, 1), (1, 0)),
    ((3, 0), (0, 2)),
    ((1, 3), (3, 3)),
    ((1, 1), (3, 1)),
    ((2, 0), (1, 2)),
    ((3, 2), (2, 3)),
    ((2, 1), (2, 2)),
)
COUNT = len(UNITS)
BASE = [64 * sum(len(unit) for unit in UNITS[:w]) for w in range(COUNT)]
PLACE = {ur: (w, i) for w, unit in enumerate(UNITS) for i, ur in enumerate(unit)}


def remote(src, dst, send, recv, device):
    return pltpu.make_async_remote_copy(
        src_ref=src,
        dst_ref=dst,
        send_sem=send,
        recv_sem=recv,
        device_id=device,
        device_id_type=pl.DeviceIdType.MESH,
    )


class Here:
    def __init__(self):
        gx = lax.axis_index("gx")
        self.gx = gx
        self.z = lax.axis_index("gy")
        self.y = gx // 8
        self.x = (gx // 2) % 4
        self.c = gx % 2

    def device(self, dy=0, dx=0, dc=0, dz=0):
        y = (self.y + dy) % 4
        x = (self.x + dx) % 4
        c = (self.c + dc) % 2
        return ((y * 4 + x) * 2 + c, (self.z + dz) % 4)

    def greet(self):
        barrier = pltpu.get_barrier_semaphore()
        partners = [dict(dz=1), dict(dz=3), dict(dz=2), dict(dc=1)]
        partners += [dict(dx=1), dict(dx=3), dict(dy=1), dict(dy=3)]
        for partner in partners:
            pl.semaphore_signal(
                barrier,
                inc=1,
                device_id=self.device(**partner),
                device_id_type=pl.DeviceIdType.MESH,
            )

    def greeted(self):
        pl.semaphore_wait(pltpu.get_barrier_semaphore(), 8)


class Projection:
    def __init__(self, here, refs, rows, sems, weight, shared=None):
        self.here = here
        self.weight = weight
        self.shared = shared
        self.rows = rows
        self.mine, self.spread, self.partial, self.far_sum, self.last, self.ready, self.owned = refs
        self.wide = self.owned.shape[2]
        self.tall = [len(unit) * (64 if shared is None else 72) for unit in UNITS]
        self.got_z, self.got_near, self.got_far = (sems.at[k] for k in range(3))
        self.got_shard = lambda u, r: sems.at[3 + u * 4 + r]
        self.got_sibling = lambda w: sems.at[19 + w]
        self.got_sum = lambda w: sems.at[19 + COUNT + w]
        self.got_last = lambda w: sems.at[19 + 2 * COUNT + w]
        self.put_z, self.put_shard, self.put_sibling, self.put_sum, self.put_near, self.put_far = (
            sems.at[19 + 3 * COUNT + k] for k in range(6)
        )

    SEMAPHORES = 25 + 3 * COUNT

    @staticmethod
    def scratch(wide, kind):
        tall = 128 if wide == 512 else 144
        return [
            pltpu.VMEM((4, 8, DEPTH), jnp.bfloat16),
            pltpu.VMEM((4, 8, DEPTH), jnp.bfloat16),
            pltpu.VMEM((COUNT, 4, tall, HD), kind),
            pltpu.VMEM((COUNT, tall, HD), kind),
            pltpu.VMEM((COUNT, 2, tall, HD), kind),
            pltpu.VMEM((COUNT, 4, 8, wide), jnp.bfloat16),
            pltpu.VMEM((32, 8, wide), jnp.bfloat16),
        ]

    def wait(self, ref, sem):
        remote(ref, ref, self.put_z, sem, self.here.device(dc=1)).wait_recv()

    def exchange(self, dz):
        z = self.here.z
        remote(
            self.mine.at[(z + dz) % 4],
            self.spread.at[z],
            self.put_z,
            self.got_z,
            self.here.device(dz=dz),
        ).start()

    def exchanged(self):
        three = self.spread.at[pl.ds(0, 3)]
        self.wait(three, self.got_z)
        for part in range(2):
            both = jnp.concatenate([self.spread[2 * part], self.spread[2 * part + 1]], axis=0)
            self.rows[pl.ds(self.start_of(0, 0, 0) + 16 * part, 16), :] = both

    @staticmethod
    def start_of(u, r, core):
        w, i = PLACE[(u, r)]
        return BASE[w] + (i * 2 + core) * 32

    def slot(self, part, u, r, half=None):
        columns = pl.ds(0, DEPTH) if half is None else pl.ds(half * (DEPTH // 2), DEPTH // 2)
        return self.rows.at[pl.ds(self.start_of(u, r, 0) + part * 16, 16), columns]

    def hop(self, u, r, first, step, half=None):
        nu, nr = (u, (r - step) % 4) if first else ((u - step) % 4, r)
        for part in range(2):
            along = dict(dx=step) if first == (part == 0) else dict(dy=step)
            remote(
                self.slot(part, u, r, half),
                self.slot(part, nu, nr, half),
                self.put_shard,
                self.got_shard(nu, nr),
                self.here.device(**along),
            ).start()

    def to_sibling(self, u, r):
        remote(
            self.rows.at[pl.ds(self.start_of(u, r, 0), 32)],
            self.rows.at[pl.ds(self.start_of(u, r, 1), 32)],
            self.put_sibling,
            self.got_sibling(PLACE[(u, r)][0]),
            self.here.device(dc=1),
        ).start()

    def start(self):
        for first in (True, False):
            self.hop(0, 0, first, 1)
            self.hop(0, 0, first, -1)
        self.to_sibling(0, 0)

    def second(self, r):
        self.hop(0, r, False, 1)
        self.hop(0, r, False, -1)

    def take(self, u, r):
        self.wait(self.rows.at[pl.ds(self.start_of(u, r, 0), 32)], self.got_shard(u, r))
        if u in (1, 3):
            self.hop(u, r, False, 1 if u == 3 else -1, 0 if u == 3 else 1)
        elif u == 0 and r in (1, 3):
            self.hop(u, r, True, 1 if r == 3 else -1, 0 if r == 3 else 1)
        self.to_sibling(u, r)

    def dots(self, w):
        pairs = len(UNITS[w])
        high = 16 * pairs
        self.wait(self.rows.at[pl.ds(BASE[w], 32 * pairs)], self.got_sibling(w))

        @pl.loop(0, 2)
        def _(n):
            out = jnp.dot(
                self.rows[pl.ds(BASE[w], 64 * pairs), :],
                self.weight[:, pl.ds(pl.multiple_of(n * 256, 256), 256)],
                preferred_element_type=jnp.float32,
            ).reshape(2 * pairs, 4, 8, 256)
            for d in range(4):
                for m in range(2):
                    block = out[:, d, :, m * HD : (m + 1) * HD].reshape(high, HD)
                    at = pl.ds(pl.multiple_of((n * 2 + m) * high, high), high)
                    self.partial[w, d, at, :] = block.astype(self.partial.dtype)

        if self.shared is not None:
            own = [self.rows[pl.ds(BASE[w] + i * 64, 32), :] for i in range(pairs)]
            out = lax.dot_general(
                jnp.concatenate(own, axis=0) if pairs > 1 else own[0],
                self.shared[...],
                (((1,), (1,)), ((), ())),
                preferred_element_type=jnp.float32,
            ).reshape(pairs, 4, 8, HD)
            for d in range(4):
                at = pl.ds(4 * high, 8 * pairs)
                self.partial[w, d, at, :] = out[:, d].reshape(8 * pairs, HD)

    def sum_copy(self, src, dst, sem, dz):
        remote(src, dst, self.put_sum, sem, self.here.device(dz=dz)).start()

    def sum_out(self, w):
        z = self.here.z
        at = pl.ds(0, self.tall[w])
        self.sum_copy(
            self.partial.at[w, (z + 2) % 4, at], self.far_sum.at[w, at], self.got_sum(w), 2
        )
        for side, dz in ((0, 1), (1, -1)):
            self.sum_copy(
                self.partial.at[w, (z + dz) % 4, at],
                self.last.at[w, side, at],
                self.got_last(w),
                dz,
            )

    def owners_out(self, w):
        here = self.here
        pairs = len(UNITS[w])
        at = pl.ds(0, self.tall[w])
        self.wait(self.last.at[w, :, at], self.got_last(w))
        total = self.partial[w, here.z, at].astype(jnp.float32)
        for side in range(2):
            total = total + self.last[w, side, at].astype(jnp.float32)
        self.wait(self.far_sum.at[w, at], self.got_sum(w))
        total = total + self.far_sum[w, at].astype(jnp.float32)
        total = total.astype(jnp.bfloat16).astype(jnp.float32)
        high = 16 * pairs
        for n in range(4):
            block = total[n * high : (n + 1) * high].reshape(2 * pairs, 8, HD)
            self.ready[w, pl.ds(0, 2 * pairs), :, pl.ds(n * HD, HD)] = block.astype(jnp.bfloat16)
        if self.shared is not None:
            for i in range(pairs):
                block = total[4 * high + i * 8 : 4 * high + i * 8 + 8]
                self.ready[w, 2 * i, :, pl.ds(512, HD)] = block.astype(jnp.bfloat16)
        for i, (u, r) in enumerate(UNITS[w]):
            for core in range(2):
                j = i * 2 + core
                if w == 0 and j == 0:
                    self.owned[here.gx] = self.ready[0, 0]
                    continue
                wide = pl.ds(0, 512 if core else self.wide)
                remote(
                    self.ready.at[w, j, :, wide],
                    self.owned.at[here.gx, :, wide],
                    self.put_far if core else self.put_near,
                    self.got_far if core else self.got_near,
                    self.owner(u, r, core),
                ).start()

    def owner(self, u, r, core):
        first = self.here.z < 2
        dy = jnp.where(first, u, r)
        dx = jnp.where(first, r, u)
        return self.here.device(dy, dx, core)

    def near(self):
        return self.owned.at[pl.ds(0, 15)]

    def far(self):
        return self.owned.at[pl.ds(0, 16), :, pl.ds(0, 512)]

    def owners_in(self):
        self.wait(self.near(), self.got_near)
        self.wait(self.far(), self.got_far)

    def unit(self, w):
        self.dots(w)
        self.sum_out(w)

    def run(self, weight_in):
        self.exchanged()
        self.start()
        self.take(0, 3)
        self.take(0, 1)
        self.second(3)
        self.second(1)
        weight_in()
        self.unit(0)
        self.take(3, 0)
        self.take(1, 0)
        self.unit(1)
        self.take(0, 2)
        self.second(2)
        self.unit(2)
        self.take(3, 3)
        self.take(1, 3)
        self.unit(3)
        self.take(3, 1)
        self.take(1, 1)
        self.owners_out(0)
        self.unit(4)
        self.take(2, 0)
        self.take(3, 2)
        self.take(1, 2)
        self.owners_out(1)
        self.unit(5)
        self.take(2, 3)
        self.unit(6)
        self.take(2, 1)
        self.take(2, 2)
        self.owners_out(2)
        self.unit(7)
        self.owners_out(3)
        self.owners_out(4)
        self.owners_out(5)
        self.owners_out(6)
        self.owners_out(7)
        self.owners_in()

    def wait_sent(self, ref, sem):
        remote(ref, ref, sem, self.got_z, self.here.device(dc=1)).wait_send()

    def finish_exchange(self):
        self.wait_sent(self.mine.at[pl.ds(0, 3)], self.put_z)

    def finish(self):
        for ref, sem in (
            (self.rows.at[pl.ds(0, 480)], self.put_shard),
            (self.rows.at[pl.ds(0, 512)], self.put_sibling),
            (self.partial.at[pl.ds(0, 6)], self.put_sum),
            (self.near(), self.put_near),
            (self.far(), self.put_far),
        ):
            self.wait_sent(ref, sem)


def normalized(step, hidden, gain):
    widened = hidden[...].astype(jnp.float32)
    scale = lax.rsqrt(jnp.mean(widened * widened, axis=-1, keepdims=True) + eps)
    for z in range(4):
        columns = pl.ds(z * DEPTH, DEPTH)
        step.mine[z] = (hidden[:, columns].astype(jnp.float32) * scale * gain[:, columns]).astype(
            jnp.bfloat16
        )


def turn(lengths, freqs, turns):
    row = lax.broadcasted_iota(jnp.int32, (ROWS, HD), 0)
    lane = lax.broadcasted_iota(jnp.int32, (ROWS, HD), 1)
    position = jnp.zeros((ROWS, HD), jnp.float32)
    for r in range(ROWS):
        position = jnp.where(row == r, lengths[r].astype(jnp.float32), position)
    angle = position * freqs[...]
    turns[0] = jnp.cos(angle)
    turns[1] = jnp.where(lane < HD // 2, -jnp.sin(angle), jnp.sin(angle))


def heads(core, owned, turns, qkv):
    for pair in range(16):
        even = owned[2 * pair, :, pl.ds(0, 512)].astype(jnp.float32)
        odd = owned[2 * pair + 1, :, pl.ds(0, 512)].astype(jnp.float32)
        between = owned[2 * pair + core, :, pl.ds(512, HD)].astype(jnp.float32)
        for t in range(9):
            if t < 4:
                head = even[:, t * HD : (t + 1) * HD]
            elif t > 4:
                head = odd[:, (t - 5) * HD : (t - 4) * HD]
            else:
                head = between
            h = pair * 9 + t
            if h < HQ + KVH:
                head = head * turns[0] + pltpu.roll(head, HD // 2, 1) * turns[1]
                head = head.astype(jnp.bfloat16).astype(jnp.float32)
            qkv[pl.ds(h * ROWS, ROWS), :] = head


def attend(z, lengths, keys, values, qkv, scored, weighed, mixed, out):
    share = HQ // KVH
    scale = 1.0 / math.sqrt(HD)
    batch = 8

    def columns(g):
        return pl.ds(pl.multiple_of((2 * z + g) * HD, HD), HD)

    def span(g, r):
        return pl.ds((2 * z + g) * share * ROWS + r, share, stride=ROWS)

    @pl.loop(0, ROWS // batch)
    def _(k):
        for b in range(batch):
            r = k * batch + b
            for g in range(2):
                scored[r, pl.ds(g * share, share), :] = (
                    lax.dot_general(
                        qkv[span(g, r), :].astype(jnp.bfloat16),
                        keys[r, :, columns(g)],
                        (((1,), (1,)), ((), ())),
                        preferred_element_type=jnp.float32,
                    )
                    * scale
                )

    @pl.loop(0, ROWS // batch)
    def _(k):
        for b in range(batch):
            r = k * batch + b
            valid = lax.broadcasted_iota(jnp.int32, (share, CACHE), 1) < lengths[r]
            for g in range(2):
                key_new = qkv[pl.ds((HQ + 2 * z + g) * ROWS + r, 1), :]
                value_new = qkv[pl.ds((HQ + KVH + 2 * z + g) * ROWS + r, 1), :]
                fresh = jnp.sum(qkv[span(g, r), :] * key_new, axis=1, keepdims=True) * scale
                scores = jnp.where(valid, scored[r, pl.ds(g * share, share), :], -jnp.inf)
                top = jnp.maximum(jnp.max(scores, axis=1, keepdims=True), fresh)
                probs = jnp.exp(scores - top)
                pnew = jnp.exp(fresh - top)
                total = jnp.sum(probs, axis=1, keepdims=True) + pnew
                weighed[r, pl.ds(g * share, share), :] = (probs / total).astype(jnp.bfloat16)
                wnew = (pnew / total).astype(jnp.bfloat16).astype(jnp.float32)
                mixed[pl.ds(g * share * ROWS + r, share, stride=ROWS), :] = wnew * value_new

    @pl.loop(0, ROWS // batch)
    def _(k):
        for b in range(batch):
            r = k * batch + b
            for g in range(2):
                at = pl.ds(g * share * ROWS + r, share, stride=ROWS)
                mixed[at, :] = mixed[at, :] + jnp.dot(
                    weighed[r, pl.ds(g * share, share), :],
                    values[r, :, columns(g)],
                    preferred_element_type=jnp.float32,
                )

    for h in range(2 * share):
        out[z, :, pl.ds(h * HD, HD)] = mixed[pl.ds(h * ROWS, ROWS), :].astype(jnp.bfloat16)


def transposed(raw, weight):
    @pl.loop(0, DEPTH // 512)
    def _(k):
        for n in range(4):
            at = pl.ds(pl.multiple_of(k * 512, 512), 512)
            weight[at, pl.ds(n * HD, HD)] = raw[pl.ds(n * HD, HD), at].T


def layer(
    lengths_in,
    hidden_in,
    gain_in,
    freqs_in,
    w_qkv,
    k_cache,
    v_cache,
    w_out,
    out,
    lengths,
    hidden,
    gain,
    freqs,
    small,
    later_rows,
    shared,
    weight_in,
    keys,
    values,
    weight_out,
    turns,
    qkv,
    scored,
    weighed,
    mixed,
    rows,
    loads,
    sems,
    *refs,
):
    here = Here()
    here.greet()
    staged = [
        pltpu.make_async_copy(hidden_in, hidden, small.at[0]),
        pltpu.make_async_copy(gain_in, gain, small.at[1]),
        pltpu.make_async_copy(freqs_in, freqs, small.at[2]),
        pltpu.make_async_copy(lengths_in, lengths, small.at[3]),
    ]
    for copy in staged:
        copy.start()
    count = len(refs) // 2
    first = Projection(here, refs[:count], rows, sems, weight_in, shared)
    second = Projection(here, refs[count:], later_rows, sems, weight_out)
    raw = later_rows.at[pl.ds(0, 512)]
    c = here.c
    half = w_qkv.at[pl.ds(pl.multiple_of((1 - c) * 512, 64), 64)]
    place = shared.at[pl.ds(pl.multiple_of(c * 64, 64), 64)]
    fetch = [
        pltpu.make_async_copy(
            w_qkv.at[pl.ds(pl.multiple_of(c * 64, 64), 512)], raw, loads.at[0]
        ),
        pltpu.make_async_copy(half, place, loads.at[1]),
        pltpu.make_async_copy(k_cache, keys, loads.at[2]),
        pltpu.make_async_copy(v_cache, values, loads.at[3]),
        pltpu.make_async_copy(w_out, weight_out, loads.at[4]),
    ]
    for copy in staged:
        copy.wait()
    for copy in fetch[:2]:
        copy.start()
    normalized(first, hidden, gain)
    here.greeted()
    for dz in (2, 1, 3):
        first.exchange(dz)
    first.spread[here.z] = first.mine[here.z]
    swap = remote(half, place, loads.at[5], loads.at[6], here.device(dc=1))
    swap.start()
    for copy in fetch[2:]:
        copy.start()
    turn(lengths, freqs, turns)
    fetch[0].wait()
    transposed(raw, weight_in)
    fetch[1].wait()
    first.run(swap.wait)
    heads(c, first.owned, turns, qkv)
    fetch[2].wait()
    fetch[3].wait()
    first.finish_exchange()
    for dz in (2, 1, 3, 0):
        to = (here.z + dz) % 4
        result = second.mine if dz else second.spread
        attend(to, lengths, keys, values, qkv, scored, weighed, mixed, result)
        if dz:
            second.exchange(dz)
    first.finish()
    second.run(fetch[4].wait)
    out[...] = second.owned[...]
    second.finish_exchange()
    second.finish()


def on_device(hidden_in, norm_gain, w_qkv, k_cache, v_cache, lengths, w_out):
    freqs = theta ** (-2.0 * (np.arange(HD) % (HD // 2)) / HD)
    freqs = jnp.asarray(freqs.astype(np.float32).reshape(1, HD))
    vmem = pl.BlockSpec(memory_space=pltpu.VMEM)
    hbm = pl.BlockSpec(memory_space=pl.ANY)
    blocks = pl.pallas_call(
        layer,
        out_shape=jax.ShapeDtypeStruct((32, ROWS, 512), jnp.bfloat16),
        in_specs=[hbm] * 8,
        out_specs=vmem,
        scratch_shapes=[
            pltpu.SMEM((ROWS,), jnp.int32),
            pltpu.VMEM((ROWS, 4 * DEPTH), jnp.bfloat16),
            pltpu.VMEM((1, 4 * DEPTH), jnp.float32),
            pltpu.VMEM((1, HD), jnp.float32),
            pltpu.SemaphoreType.DMA((4,)),
            pltpu.VMEM((1024, DEPTH), jnp.bfloat16),
            pltpu.VMEM((HD, DEPTH), jnp.bfloat16),
            pltpu.VMEM((DEPTH, 512), jnp.bfloat16),
            pltpu.VMEM((ROWS, CACHE, KVH * HD), jnp.bfloat16),
            pltpu.VMEM((ROWS, CACHE, KVH * HD), jnp.bfloat16),
            pltpu.VMEM((DEPTH, 512), jnp.bfloat16),
            pltpu.VMEM((2, ROWS, HD), jnp.float32),
            pltpu.VMEM(((HQ + 2 * KVH) * ROWS, HD), jnp.float32),
            pltpu.VMEM((ROWS, HQ // 4, CACHE), jnp.float32),
            pltpu.VMEM((ROWS, HQ // 4, CACHE), jnp.bfloat16),
            pltpu.VMEM((HQ // 4 * ROWS, HD), jnp.float32),
            pltpu.VMEM((1024, DEPTH), jnp.bfloat16),
            pltpu.SemaphoreType.DMA((7,)),
            pltpu.SemaphoreType.DMA((Projection.SEMAPHORES,)),
        ]
        + Projection.scratch(QWIDE, jnp.float32)
        + Projection.scratch(512, jnp.bfloat16),
        compiler_params=pltpu.CompilerParams(
            collective_id=0, has_side_effects=True, vmem_limit_bytes=60 * 1024 * 1024
        ),
        name="layer",
    )(lengths, hidden_in, norm_gain.reshape(1, -1), freqs, w_qkv.T, k_cache, v_cache, w_out)
    return blocks.transpose(1, 0, 2).reshape(ROWS, 32 * 512)


def solution(mesh):
    return jax.shard_map(
        on_device,
        mesh=mesh,
        in_specs=(
            P(("gx", "gy"), None),
            P(),
            P("gy", "gx"),
            P(("gx", "gy"), None, None),
            P(("gx", "gy"), None, None),
            P(("gx", "gy")),
            P("gy", "gx"),
        ),
        out_specs=P(("gx", "gy"), None),
        check_vma=False,
    )
```

```python
import math

import jax
import jax.numpy as jnp
import numpy as np
from jax import lax
from jax.experimental import pallas as pl
from jax.experimental.pallas import tpu as pltpu
from jax.sharding import PartitionSpec as P

HQ = 128
KVH = 8
HD = 128
ROWS = 8
CACHE = 512
DEPTH = 4096
QWIDE = 640

eps = 1e-05
theta = 500000.0

UNITS = (
    ((0, 0), (0, 3)),
    ((0, 1), (1, 0)),
    ((3, 0), (0, 2)),
    ((1, 3), (3, 3)),
    ((1, 1), (3, 1)),
    ((2, 0), (1, 2)),
    ((3, 2), (2, 3)),
    ((2, 1), (2, 2)),
)
COUNT = len(UNITS)
BASE = [64 * sum(len(unit) for unit in UNITS[:w]) for w in range(COUNT)]
PLACE = {ur: (w, i) for w, unit in enumerate(UNITS) for i, ur in enumerate(unit)}


def remote(src, dst, send, recv, device):
    return pltpu.make_async_remote_copy(
        src_ref=src,
        dst_ref=dst,
        send_sem=send,
        recv_sem=recv,
        device_id=device,
        device_id_type=pl.DeviceIdType.MESH,
    )


class Here:
    def __init__(self):
        gx = lax.axis_index("gx")
        self.gx = gx
        self.z = lax.axis_index("gy")
        self.y = gx // 8
        self.x = (gx // 2) % 4
        self.c = gx % 2

    def device(self, dy=0, dx=0, dc=0, dz=0):
        y = (self.y + dy) % 4
        x = (self.x + dx) % 4
        c = (self.c + dc) % 2
        return ((y * 4 + x) * 2 + c, (self.z + dz) % 4)

    def greet(self):
        barrier = pltpu.get_barrier_semaphore()
        partners = [dict(dz=1), dict(dz=3), dict(dz=2), dict(dc=1)]
        partners += [dict(dx=1), dict(dx=3), dict(dy=1), dict(dy=3)]
        for partner in partners:
            pl.semaphore_signal(
                barrier,
                inc=1,
                device_id=self.device(**partner),
                device_id_type=pl.DeviceIdType.MESH,
            )

    def greeted(self):
        pl.semaphore_wait(pltpu.get_barrier_semaphore(), 8)


class Projection:
    def __init__(self, here, refs, rows, sems, weight, shared=None):
        self.here = here
        self.weight = weight
        self.shared = shared
        self.rows = rows
        self.mine, self.spread, self.partial, self.far_sum, self.last, self.ready, self.owned = refs
        self.wide = self.owned.shape[2]
        self.tall = [len(unit) * (64 if shared is None else 72) for unit in UNITS]
        self.got_z, self.got_near, self.got_far = (sems.at[k] for k in range(3))
        self.got_shard = lambda u, r: sems.at[3 + u * 4 + r]
        self.got_sibling = lambda w: sems.at[19 + w]
        self.got_sum = lambda w: sems.at[19 + COUNT + w]
        self.got_last = lambda w: sems.at[19 + 2 * COUNT + w]
        self.put_z, self.put_shard, self.put_sibling, self.put_sum, self.put_near, self.put_far = (
            sems.at[19 + 3 * COUNT + k] for k in range(6)
        )

    SEMAPHORES = 25 + 3 * COUNT

    @staticmethod
    def scratch(wide, kind):
        tall = 128 if wide == 512 else 144
        return [
            pltpu.VMEM((4, 8, DEPTH), jnp.bfloat16),
            pltpu.VMEM((4, 8, DEPTH), jnp.bfloat16),
            pltpu.VMEM((COUNT, 4, tall, HD), kind),
            pltpu.VMEM((COUNT, tall, HD), kind),
            pltpu.VMEM((COUNT, 2, tall, HD), kind),
            pltpu.VMEM((COUNT, 4, 8, wide), jnp.bfloat16),
            pltpu.VMEM((32, 8, wide), jnp.bfloat16),
        ]

    def wait(self, ref, sem):
        remote(ref, ref, self.put_z, sem, self.here.device(dc=1)).wait_recv()

    def exchange(self, dz):
        z = self.here.z
        remote(
            self.mine.at[(z + dz) % 4],
            self.spread.at[z],
            self.put_z,
            self.got_z,
            self.here.device(dz=dz),
        ).start()

    def exchanged(self):
        three = self.spread.at[pl.ds(0, 3)]
        self.wait(three, self.got_z)
        for part in range(2):
            both = jnp.concatenate([self.spread[2 * part], self.spread[2 * part + 1]], axis=0)
            self.rows[pl.ds(self.start_of(0, 0, 0) + 16 * part, 16), :] = both

    @staticmethod
    def start_of(u, r, core):
        w, i = PLACE[(u, r)]
        return BASE[w] + (i * 2 + core) * 32

    def slot(self, part, u, r, half=None):
        columns = pl.ds(0, DEPTH) if half is None else pl.ds(half * (DEPTH // 2), DEPTH // 2)
        return self.rows.at[pl.ds(self.start_of(u, r, 0) + part * 16, 16), columns]

    def hop(self, u, r, first, step, half=None):
        nu, nr = (u, (r - step) % 4) if first else ((u - step) % 4, r)
        for part in range(2):
            along = dict(dx=step) if first == (part == 0) else dict(dy=step)
            remote(
                self.slot(part, u, r, half),
                self.slot(part, nu, nr, half),
                self.put_shard,
                self.got_shard(nu, nr),
                self.here.device(**along),
            ).start()

    def to_sibling(self, u, r):
        remote(
            self.rows.at[pl.ds(self.start_of(u, r, 0), 32)],
            self.rows.at[pl.ds(self.start_of(u, r, 1), 32)],
            self.put_sibling,
            self.got_sibling(PLACE[(u, r)][0]),
            self.here.device(dc=1),
        ).start()

    def start(self):
        for first in (True, False):
            self.hop(0, 0, first, 1)
            self.hop(0, 0, first, -1)
        self.to_sibling(0, 0)

    def second(self, r):
        self.hop(0, r, False, 1)
        self.hop(0, r, False, -1)

    def take(self, u, r):
        self.wait(self.rows.at[pl.ds(self.start_of(u, r, 0), 32)], self.got_shard(u, r))
        if u in (1, 3):
            self.hop(u, r, False, 1 if u == 3 else -1, 0 if u == 3 else 1)
        elif u == 0 and r in (1, 3):
            self.hop(u, r, True, 1 if r == 3 else -1, 0 if r == 3 else 1)
        self.to_sibling(u, r)

    def dots(self, w):
        pairs = len(UNITS[w])
        high = 16 * pairs
        self.wait(self.rows.at[pl.ds(BASE[w], 32 * pairs)], self.got_sibling(w))

        @pl.loop(0, 2)
        def _(n):
            out = jnp.dot(
                self.rows[pl.ds(BASE[w], 64 * pairs), :],
                self.weight[:, pl.ds(pl.multiple_of(n * 256, 256), 256)],
                preferred_element_type=jnp.float32,
            ).reshape(2 * pairs, 4, 8, 256)
            for d in range(4):
                for m in range(2):
                    block = out[:, d, :, m * HD : (m + 1) * HD].reshape(high, HD)
                    at = pl.ds(pl.multiple_of((n * 2 + m) * high, high), high)
                    self.partial[w, d, at, :] = block.astype(self.partial.dtype)

        if self.shared is not None:
            own = [self.rows[pl.ds(BASE[w] + i * 64, 32), :] for i in range(pairs)]
            out = lax.dot_general(
                jnp.concatenate(own, axis=0) if pairs > 1 else own[0],
                self.shared[...],
                (((1,), (1,)), ((), ())),
                preferred_element_type=jnp.float32,
            ).reshape(pairs, 4, 8, HD)
            for d in range(4):
                at = pl.ds(4 * high, 8 * pairs)
                self.partial[w, d, at, :] = out[:, d].reshape(8 * pairs, HD)

    def sum_copy(self, src, dst, sem, dz):
        remote(src, dst, self.put_sum, sem, self.here.device(dz=dz)).start()

    def sum_out(self, w):
        z = self.here.z
        at = pl.ds(0, self.tall[w])
        self.sum_copy(
            self.partial.at[w, (z + 2) % 4, at], self.far_sum.at[w, at], self.got_sum(w), 2
        )
        for side, dz in ((0, 1), (1, -1)):
            self.sum_copy(
                self.partial.at[w, (z + dz) % 4, at],
                self.last.at[w, side, at],
                self.got_last(w),
                dz,
            )

    def owners_out(self, w):
        here = self.here
        pairs = len(UNITS[w])
        at = pl.ds(0, self.tall[w])
        self.wait(self.last.at[w, :, at], self.got_last(w))
        total = self.partial[w, here.z, at].astype(jnp.float32)
        for side in range(2):
            total = total + self.last[w, side, at].astype(jnp.float32)
        self.wait(self.far_sum.at[w, at], self.got_sum(w))
        total = total + self.far_sum[w, at].astype(jnp.float32)
        total = total.astype(jnp.bfloat16).astype(jnp.float32)
        high = 16 * pairs
        for n in range(4):
            block = total[n * high : (n + 1) * high].reshape(2 * pairs, 8, HD)
            self.ready[w, pl.ds(0, 2 * pairs), :, pl.ds(n * HD, HD)] = block.astype(jnp.bfloat16)
        if self.shared is not None:
            for i in range(pairs):
                block = total[4 * high + i * 8 : 4 * high + i * 8 + 8]
                self.ready[w, 2 * i, :, pl.ds(512, HD)] = block.astype(jnp.bfloat16)
        for i, (u, r) in enumerate(UNITS[w]):
            for core in range(2):
                j = i * 2 + core
                if w == 0 and j == 0:
                    self.owned[here.gx] = self.ready[0, 0]
                    continue
                wide = pl.ds(0, 512 if core else self.wide)
                remote(
                    self.ready.at[w, j, :, wide],
                    self.owned.at[here.gx, :, wide],
                    self.put_far if core else self.put_near,
                    self.got_far if core else self.got_near,
                    self.owner(u, r, core),
                ).start()

    def owner(self, u, r, core):
        first = self.here.z < 2
        dy = jnp.where(first, u, r)
        dx = jnp.where(first, r, u)
        return self.here.device(dy, dx, core)

    def near(self):
        return self.owned.at[pl.ds(0, 15)]

    def far(self):
        return self.owned.at[pl.ds(0, 16), :, pl.ds(0, 512)]

    def owners_in(self):
        self.wait(self.near(), self.got_near)
        self.wait(self.far(), self.got_far)

    def unit(self, w):
        self.dots(w)
        self.sum_out(w)

    def run(self, weight_in):
        self.exchanged()
        self.start()
        self.take(0, 3)
        self.take(0, 1)
        self.second(3)
        self.second(1)
        weight_in()
        self.unit(0)
        self.take(3, 0)
        self.take(1, 0)
        self.unit(1)
        self.take(0, 2)
        self.second(2)
        self.unit(2)
        self.take(3, 3)
        self.take(1, 3)
        self.unit(3)
        self.take(3, 1)
        self.take(1, 1)
        self.owners_out(0)
        self.unit(4)
        self.take(2, 0)
        self.take(3, 2)
        self.take(1, 2)
        self.owners_out(1)
        self.unit(5)
        self.take(2, 3)
        self.unit(6)
        self.take(2, 1)
        self.take(2, 2)
        self.owners_out(2)
        self.unit(7)
        self.owners_out(3)
        self.owners_out(4)
        self.owners_out(5)
        self.owners_out(6)
        self.owners_out(7)
        self.owners_in()

    def wait_sent(self, ref, sem):
        remote(ref, ref, sem, self.got_z, self.here.device(dc=1)).wait_send()

    def finish_exchange(self):
        self.wait_sent(self.mine.at[pl.ds(0, 3)], self.put_z)

    def finish(self):
        for ref, sem in (
            (self.rows.at[pl.ds(0, 480)], self.put_shard),
            (self.rows.at[pl.ds(0, 512)], self.put_sibling),
            (self.partial.at[pl.ds(0, 6)], self.put_sum),
            (self.near(), self.put_near),
            (self.far(), self.put_far),
        ):
            self.wait_sent(ref, sem)


def normalized(step, hidden, gain):
    widened = hidden[...].astype(jnp.float32)
    scale = lax.rsqrt(jnp.mean(widened * widened, axis=-1, keepdims=True) + eps)
    for z in range(4):
        columns = pl.ds(z * DEPTH, DEPTH)
        step.mine[z] = (hidden[:, columns].astype(jnp.float32) * scale * gain[:, columns]).astype(
            jnp.bfloat16
        )


def turn(lengths, freqs, turns):
    row = lax.broadcasted_iota(jnp.int32, (ROWS, HD), 0)
    lane = lax.broadcasted_iota(jnp.int32, (ROWS, HD), 1)
    position = jnp.zeros((ROWS, HD), jnp.float32)
    for r in range(ROWS):
        position = jnp.where(row == r, lengths[r].astype(jnp.float32), position)
    angle = position * freqs[...]
    turns[0] = jnp.cos(angle)
    turns[1] = jnp.where(lane < HD // 2, -jnp.sin(angle), jnp.sin(angle))


def heads(core, owned, turns, qkv):
    for pair in range(16):
        even = owned[2 * pair, :, pl.ds(0, 512)].astype(jnp.float32)
        odd = owned[2 * pair + 1, :, pl.ds(0, 512)].astype(jnp.float32)
        between = owned[2 * pair + core, :, pl.ds(512, HD)].astype(jnp.float32)
        for t in range(9):
            if t < 4:
                head = even[:, t * HD : (t + 1) * HD]
            elif t > 4:
                head = odd[:, (t - 5) * HD : (t - 4) * HD]
            else:
                head = between
            h = pair * 9 + t
            if h < HQ + KVH:
                head = head * turns[0] + pltpu.roll(head, HD // 2, 1) * turns[1]
                head = head.astype(jnp.bfloat16).astype(jnp.float32)
            qkv[pl.ds(h * ROWS, ROWS), :] = head


def attend(z, lengths, keys, values, qkv, scored, weighed, mixed, out):
    share = HQ // KVH
    scale = 1.0 / math.sqrt(HD)
    batch = 8

    def columns(g):
        return pl.ds(pl.multiple_of((2 * z + g) * HD, HD), HD)

    def span(g, r):
        return pl.ds((2 * z + g) * share * ROWS + r, share, stride=ROWS)

    @pl.loop(0, ROWS // batch)
    def _(k):
        for b in range(batch):
            r = k * batch + b
            for g in range(2):
                scored[r, pl.ds(g * share, share), :] = (
                    lax.dot_general(
                        qkv[span(g, r), :].astype(jnp.bfloat16),
                        keys[r, :, columns(g)],
                        (((1,), (1,)), ((), ())),
                        preferred_element_type=jnp.float32,
                    )
                    * scale
                )

    @pl.loop(0, ROWS // batch)
    def _(k):
        for b in range(batch):
            r = k * batch + b
            valid = lax.broadcasted_iota(jnp.int32, (share, CACHE), 1) < lengths[r]
            for g in range(2):
                key_new = qkv[pl.ds((HQ + 2 * z + g) * ROWS + r, 1), :]
                value_new = qkv[pl.ds((HQ + KVH + 2 * z + g) * ROWS + r, 1), :]
                fresh = jnp.sum(qkv[span(g, r), :] * key_new, axis=1, keepdims=True) * scale
                scores = jnp.where(valid, scored[r, pl.ds(g * share, share), :], -jnp.inf)
                top = jnp.maximum(jnp.max(scores, axis=1, keepdims=True), fresh)
                probs = jnp.exp(scores - top)
                pnew = jnp.exp(fresh - top)
                total = jnp.sum(probs, axis=1, keepdims=True) + pnew
                weighed[r, pl.ds(g * share, share), :] = (probs / total).astype(jnp.bfloat16)
                wnew = (pnew / total).astype(jnp.bfloat16).astype(jnp.float32)
                mixed[pl.ds(g * share * ROWS + r, share, stride=ROWS), :] = wnew * value_new

    @pl.loop(0, ROWS // batch)
    def _(k):
        for b in range(batch):
            r = k * batch + b
            for g in range(2):
                at = pl.ds(g * share * ROWS + r, share, stride=ROWS)
                mixed[at, :] = mixed[at, :] + jnp.dot(
                    weighed[r, pl.ds(g * share, share), :],
                    values[r, :, columns(g)],
                    preferred_element_type=jnp.float32,
                )

    for h in range(2 * share):
        out[z, :, pl.ds(h * HD, HD)] = mixed[pl.ds(h * ROWS, ROWS), :].astype(jnp.bfloat16)


def transposed(raw, weight):
    @pl.loop(0, DEPTH // 512)
    def _(k):
        for n in range(4):
            at = pl.ds(pl.multiple_of(k * 512, 512), 512)
            weight[at, pl.ds(n * HD, HD)] = raw[pl.ds(n * HD, HD), at].T


def layer(
    lengths_in,
    hidden_in,
    gain_in,
    freqs_in,
    w_qkv,
    k_cache,
    v_cache,
    w_out,
    out,
    lengths,
    hidden,
    gain,
    freqs,
    small,
    later_rows,
    shared,
    weight_in,
    keys,
    values,
    weight_out,
    turns,
    qkv,
    scored,
    weighed,
    mixed,
    rows,
    loads,
    sems,
    *refs,
):
    here = Here()
    here.greet()
    staged = [
        pltpu.make_async_copy(hidden_in, hidden, small.at[0]),
        pltpu.make_async_copy(gain_in, gain, small.at[1]),
        pltpu.make_async_copy(freqs_in, freqs, small.at[2]),
        pltpu.make_async_copy(lengths_in, lengths, small.at[3]),
    ]
    for copy in staged:
        copy.start()
    count = len(refs) // 2
    first = Projection(here, refs[:count], rows, sems, weight_in, shared)
    second = Projection(here, refs[count:], later_rows, sems, weight_out)
    raw = later_rows.at[pl.ds(0, 512)]
    c = here.c
    half = w_qkv.at[pl.ds(pl.multiple_of((1 - c) * 512, 64), 64)]
    place = shared.at[pl.ds(pl.multiple_of(c * 64, 64), 64)]
    fetch = [
        pltpu.make_async_copy(
            w_qkv.at[pl.ds(pl.multiple_of(c * 64, 64), 512)], raw, loads.at[0]
        ),
        pltpu.make_async_copy(half, place, loads.at[1]),
        pltpu.make_async_copy(k_cache, keys, loads.at[2]),
        pltpu.make_async_copy(v_cache, values, loads.at[3]),
        pltpu.make_async_copy(w_out, weight_out, loads.at[4]),
    ]
    for copy in staged:
        copy.wait()
    for copy in fetch[:2]:
        copy.start()
    normalized(first, hidden, gain)
    here.greeted()
    for dz in (2, 1, 3):
        first.exchange(dz)
    first.spread[here.z] = first.mine[here.z]
    swap = remote(half, place, loads.at[5], loads.at[6], here.device(dc=1))
    swap.start()
    for copy in fetch[2:]:
        copy.start()
    turn(lengths, freqs, turns)
    fetch[0].wait()
    transposed(raw, weight_in)
    fetch[1].wait()
    first.run(swap.wait)
    heads(c, first.owned, turns, qkv)
    fetch[2].wait()
    fetch[3].wait()
    first.finish_exchange()
    for dz in (2, 1, 3, 0):
        to = (here.z + dz) % 4
        result = second.mine if dz else second.spread
        attend(to, lengths, keys, values, qkv, scored, weighed, mixed, result)
        if dz:
            second.exchange(dz)
    first.finish()
    second.run(fetch[4].wait)
    out[...] = second.owned[...].astype(jnp.float32)
    second.finish_exchange()
    second.finish()


def on_device(hidden_in, norm_gain, w_qkv, k_cache, v_cache, lengths, w_out):
    freqs = theta ** (-2.0 * (np.arange(HD) % (HD // 2)) / HD)
    freqs = jnp.asarray(freqs.astype(np.float32).reshape(1, HD))
    vmem = pl.BlockSpec(memory_space=pltpu.VMEM)
    hbm = pl.BlockSpec(memory_space=pl.ANY)
    blocks = pl.pallas_call(
        layer,
        out_shape=jax.ShapeDtypeStruct((32, ROWS, 512), jnp.float32),
        in_specs=[hbm] * 8,
        out_specs=vmem,
        scratch_shapes=[
            pltpu.SMEM((ROWS,), jnp.int32),
            pltpu.VMEM((ROWS, 4 * DEPTH), jnp.bfloat16),
            pltpu.VMEM((1, 4 * DEPTH), jnp.float32),
            pltpu.VMEM((1, HD), jnp.float32),
            pltpu.SemaphoreType.DMA((4,)),
            pltpu.VMEM((1024, DEPTH), jnp.bfloat16),
            pltpu.VMEM((HD, DEPTH), jnp.bfloat16),
            pltpu.VMEM((DEPTH, 512), jnp.bfloat16),
            pltpu.VMEM((ROWS, CACHE, KVH * HD), jnp.bfloat16),
            pltpu.VMEM((ROWS, CACHE, KVH * HD), jnp.bfloat16),
            pltpu.VMEM((DEPTH, 512), jnp.bfloat16),
            pltpu.VMEM((2, ROWS, HD), jnp.float32),
            pltpu.VMEM(((HQ + 2 * KVH) * ROWS, HD), jnp.float32),
            pltpu.VMEM((ROWS, HQ // 4, CACHE), jnp.float32),
            pltpu.VMEM((ROWS, HQ // 4, CACHE), jnp.bfloat16),
            pltpu.VMEM((HQ // 4 * ROWS, HD), jnp.float32),
            pltpu.VMEM((1024, DEPTH), jnp.bfloat16),
            pltpu.SemaphoreType.DMA((7,)),
            pltpu.SemaphoreType.DMA((Projection.SEMAPHORES,)),
        ]
        + Projection.scratch(QWIDE, jnp.float32)
        + Projection.scratch(512, jnp.bfloat16),
        compiler_params=pltpu.CompilerParams(
            collective_id=0, has_side_effects=True, vmem_limit_bytes=60 * 1024 * 1024
        ),
        name="layer",
    )(lengths, hidden_in, norm_gain.reshape(1, -1), freqs, w_qkv.T, k_cache, v_cache, w_out)
    return blocks.transpose(1, 0, 2).reshape(ROWS, 32 * 512).astype(jnp.bfloat16)


def solution(mesh):
    return jax.shard_map(
        on_device,
        mesh=mesh,
        in_specs=(
            P(("gx", "gy"), None),
            P(),
            P("gy", "gx"),
            P(("gx", "gy"), None, None),
            P(("gx", "gy"), None, None),
            P(("gx", "gy")),
            P("gy", "gx"),
        ),
        out_specs=P(("gx", "gy"), None),
        check_vma=False,
    )
```
